128 devices in a mesh: grp: 4 (over x_hi, core), dev: 32 (over y, x_lo, z).
Axes of the slice: x: 4 (x_hi: 2, x_lo: 2; x = x_hi * 2 + x_lo), y: 4, z: 4, core: 2. Of those that a mesh axis runs over, the one named last changes fastest.
Arguments:
- queries: bfloat16 [512, 4, 8192], P(('grp', 'dev')), may hold values from -6 to 6
- prefix_kv: bfloat16 [4, 16384, 2, 512], P('grp', 'dev'), may hold values from -8 to 8
- pool: bfloat16 [3072, 2, 128, 512], P(('grp', 'dev')), may hold values from -8 to 8
- new_kv: bfloat16 [512, 4, 2, 512], P(('grp', 'dev')), may hold values from -16 to 16
- unique_len: int32 [512], P(('grp', 'dev')), may hold values from 1 to 768, as said below
- page_table: int32 [128, 24], P(('grp', 'dev')), may hold values from 0 to 23, each once within a row
- send_slots: int32 [128, 24], P(('grp', 'dev')), may hold values from 0 to 23, each once within a row
Outputs:
- attended: bfloat16 [512, 4, 8192], P(('grp', 'dev'))
The draws below stay inside these ranges and needn't reach their ends.
Inputs may be any that keep to these rules, and one draw needn't show every extreme that they name: `unique_len`: some request has exactly 768 tokens. `page_table`: each row is a permutation. `send_slots`: each row is a permutation.
All inputs are finite; a program needn't handle non-finite values.
Results may differ from the reference program's by a relative error of at most 0.024.
Values may be sent and summed in bfloat16 or wider, within the bound.
No kernel may reach another device: no remote copies, remote signals or barrier semaphores. Data moves between devices by JAX's collectives and lax.ppermute only.
A program may use at most 192 MiB of HBM per device.

```python
import math
import jax
import jax.numpy as jnp
from jax import lax

HQ = 64
KVH = 4
HD = 128
GQA = 16
STEPS = 4
PAGE = 128
MAXP = 6
PREFIX = 16384
REQ_DEV = 4
REQUESTS = 512
CAPG = 6
POOL_DEV = 24
N_GRP = 4
N_DEV = 32


def draw_queries(key, part):
    key = jax.random.fold_in(key, 12)
    base_key = jax.random.fold_in(key, 0)
    full_shape = (REQUESTS, STEPS, HQ, HD)
    values = jnp.clip(jax.random.normal(base_key, full_shape, jnp.float32), -6.0, 6.0)
    return values.reshape(REQUESTS, STEPS, HQ * HD).astype(jnp.bfloat16)


def draw_prefix_kv(key, part):
    key = jax.random.fold_in(key, 11)
    base_key = jax.random.fold_in(key, 0)
    full_shape = (N_GRP, PREFIX, 2, KVH * HD)
    values = jnp.clip(2.0 * jax.random.normal(base_key, full_shape, jnp.float32), -8.0, 8.0)
    return values.astype(jnp.bfloat16)


def draw_unique_len(key, part):
    key = jax.random.fold_in(key, 13)
    level_key, drop_key, tail_key, pick_key = jax.random.split(key, 4)
    readers = REQUESTS // REQ_DEV
    levels = jax.random.randint(level_key, (readers, 1), 1, MAXP + 1)
    chosen = jax.random.randint(pick_key, (), 0, readers)
    reader_ids = jnp.arange(readers)[:, None]
    levels = jnp.where(reader_ids == chosen, MAXP, levels)
    request_ids = jnp.arange(REQ_DEV)[None, :]
    drops = jax.random.randint(drop_key, (readers, REQ_DEV), 0, 2)
    drops = jnp.where(request_ids == 0, 0, drops)
    page_count = jnp.maximum(levels - drops, 1)
    tails = jax.random.randint(tail_key, (readers, REQ_DEV), 1, PAGE + 1)
    tails = jnp.where((reader_ids == chosen) & (request_ids == 0), PAGE, tails)
    lengths = PAGE * (page_count - 1) + tails
    return lengths.reshape(REQUESTS).astype(jnp.int32)


def shard_levels(own_key, dims, cuts, smallest, high):
    gain, own = 1.0, jax.random.fold_in(own_key, 6)
    for axis_at, parts in cuts:
        steps = jnp.exp(jax.random.uniform(jax.random.fold_in(own, axis_at), (parts,), jnp.float32, smallest / len(cuts), high / len(cuts)))
        gain = gain * jnp.repeat(steps, dims[axis_at] // parts).reshape([-1 if axis == axis_at else 1 for axis in range(len(dims))])
    return gain


def bell_draw(stream_key, shape, width, bound, pieces=(), kind=jnp.bfloat16):
    values = jax.random.normal(stream_key, shape, jnp.float32) * width
    if len(pieces) > 0:
        values = shard_levels(stream_key, shape, pieces, -0.22, 0.18) * values
    return jnp.clip(values, min=-bound, max=bound).astype(kind)


def setup_inputs(seed: int = 0) -> dict:
    streams_of = jax.random.split(jax.random.key(seed), 8)
    return {
        "queries": draw_queries(jax.random.fold_in(streams_of[7], 71), 0),
        "prefix_kv": draw_prefix_kv(jax.random.fold_in(streams_of[7], 71), 0),
        "pool": bell_draw(streams_of[2], (N_GRP * N_DEV * POOL_DEV, 2, PAGE, KVH * HD), 2.0, 8.0, ((0, 128),)),
        "new_kv": bell_draw(streams_of[3], (REQUESTS, STEPS, 2, KVH * HD), 4.0, 16.0, ((0, 128),)),
        "unique_len": draw_unique_len(jax.random.fold_in(streams_of[7], 71), 0),
        "page_table": jax.vmap(lambda own: jax.random.permutation(own, REQ_DEV * MAXP))(jax.random.split(streams_of[5], (N_GRP * N_DEV))).reshape((N_GRP * N_DEV, REQ_DEV * MAXP)).astype(jnp.int32),
        "send_slots": jax.vmap(lambda own: jax.random.permutation(own, POOL_DEV))(jax.random.split(streams_of[6], (N_GRP * N_DEV))).reshape((N_GRP * N_DEV, POOL_DEV)).astype(jnp.int32),
    }


LOWEST_SCORE = -1e+30

def rounded(weights):
    return lax.optimization_barrier(weights.astype(jnp.bfloat16)).astype(jnp.float32)

def device_block(device_id, queries, prefix_kv, pool, new_kv, unique_len, page_table, send_slots):
    group_id = device_id // N_DEV
    dev_id = device_id % N_DEV
    row_count = STEPS * GQA
    scaling = 1.0 / math.sqrt(HD)
    queried = lax.dynamic_slice_in_dim(queries, device_id * REQ_DEV, REQ_DEV, 0)
    queried = queried.reshape(REQ_DEV, STEPS, KVH, GQA, HD).transpose(2, 0, 1, 3, 4)
    queried = queried.reshape(KVH, REQ_DEV, row_count, HD).astype(jnp.float32)
    prefix_rows = lax.dynamic_index_in_dim(prefix_kv, group_id, 0, keepdims=False)
    prefix_keys = prefix_rows[:, 0].reshape(PREFIX, KVH, HD).astype(jnp.float32)
    prefix_vals = prefix_rows[:, 1].reshape(PREFIX, KVH, HD).astype(jnp.float32)
    prefix_score = jnp.einsum('krqd,tkd->krqt', queried, prefix_keys) * scaling
    table_rows = lax.dynamic_index_in_dim(page_table, device_id, 0, keepdims=False).reshape(REQ_DEV, MAXP)
    sender = table_rows // CAPG * N_DEV + dev_id
    slot_ids = group_id * CAPG + table_rows % CAPG
    local_pages = send_slots[sender, slot_ids]
    fetched = pool[sender * POOL_DEV + local_pages]
    own_keys = fetched[:, :, 0].reshape(REQ_DEV, MAXP * PAGE, KVH, HD).astype(jnp.float32)
    own_vals = fetched[:, :, 1].reshape(REQ_DEV, MAXP * PAGE, KVH, HD).astype(jnp.float32)
    lengths = lax.dynamic_slice_in_dim(unique_len, device_id * REQ_DEV, REQ_DEV, 0)
    alive = jnp.arange(MAXP * PAGE, dtype=jnp.int32)[None, :] < lengths[:, None]
    own_score = jnp.einsum('krqd,rtkd->krqt', queried, own_keys) * scaling
    own_score = jnp.where(alive[None, :, None, :], own_score, LOWEST_SCORE)
    fresh = lax.dynamic_slice_in_dim(new_kv, device_id * REQ_DEV, REQ_DEV, 0)
    fresh_keys = fresh[:, :, 0].reshape(REQ_DEV, STEPS, KVH, HD).astype(jnp.float32)
    fresh_vals = fresh[:, :, 1].reshape(REQ_DEV, STEPS, KVH, HD).astype(jnp.float32)
    causal = jnp.arange(row_count, dtype=jnp.int32)[:, None] // GQA >= jnp.arange(STEPS, dtype=jnp.int32)[None, :]
    fresh_score = jnp.einsum('krqd,rtkd->krqt', queried, fresh_keys) * scaling
    fresh_score = jnp.where(causal[None, None], fresh_score, LOWEST_SCORE)
    highest = jnp.maximum(jnp.maximum(prefix_score.max(-1), own_score.max(-1)), fresh_score.max(-1))
    prefix_w = jnp.exp(prefix_score - highest[..., None])
    own_w = jnp.exp(own_score - highest[..., None])
    fresh_w = jnp.exp(fresh_score - highest[..., None])
    weight_sum = prefix_w.sum(-1) + own_w.sum(-1) + fresh_w.sum(-1)
    weighted = jnp.einsum('krqt,tkd->krqd', rounded(prefix_w), prefix_vals)
    weighted = weighted + jnp.einsum('krqt,rtkd->krqd', rounded(own_w), own_vals)
    weighted = weighted + jnp.einsum('krqt,rtkd->krqd', rounded(fresh_w), fresh_vals)
    result = weighted / weight_sum[..., None]
    result = result.reshape(KVH, REQ_DEV, STEPS, GQA, HD).transpose(1, 2, 0, 3, 4)
    return result.reshape(REQ_DEV, STEPS, HQ * HD).astype(jnp.bfloat16)

def reference(queries, prefix_kv, pool, new_kv, unique_len, page_table, send_slots):

    def one_device(device_id):
        return device_block(device_id, queries, prefix_kv, pool, new_kv, unique_len, page_table, send_slots)
    blocks = lax.map(one_device, jnp.arange(N_GRP * N_DEV, dtype=jnp.int32))
    return blocks.reshape(REQUESTS, STEPS, HQ * HD)
```

```python
import functools
import math

import jax
import jax.numpy as jnp
from jax import lax
from jax.experimental import pallas as pl
from jax.experimental.pallas import tpu as pltpu
from jax.sharding import Mesh, PartitionSpec as P

HQ = 64
KVH = 4
HD = 128
GQA = 16
STEPS = 4
PAGE = 128
MAXP = 6
REQ = 4
RS = REQ * STEPS
ROWS = RS * GQA
PACK = ROWS + 16
FLOOR = -1e29
LOWEST = -1e30
LOG2 = math.log2(math.e) / math.sqrt(HD)
AXES = ("grp", "y", "xl", "z")
F32 = jnp.float32
BF16 = jnp.bfloat16


def dot_t(a, b):
    return lax.dot_general(a, b, (((1,), (1,)), ((), ())), preferred_element_type=F32)


def split3(x):
    hi = x.astype(BF16).astype(F32)
    rest = x - hi
    mid = rest.astype(BF16).astype(F32)
    return hi, mid, rest - mid


def pack_stats(m, l):
    lane = lax.broadcasted_iota(jnp.int32, (128, 128), 1)
    parts = []
    for half in range(2):
        rows = slice(half * 128, half * 128 + 128)
        cols = split3(m[rows]) + split3(l[rows])
        stats = jnp.zeros((128, 128), F32)
        for i, col in enumerate(cols):
            stats = jnp.where(lane == i, jnp.broadcast_to(col, (128, 128)), stats)
        parts.append(stats.T[:8])
    return jnp.concatenate(parts, axis=0).astype(BF16)


def unpack_stats(packed):
    wide = packed.astype(F32)
    ms, ls = [], []
    for half in range(2):
        tall = jnp.concatenate(
            [wide[half * 8 : half * 8 + 8], jnp.zeros((120, 128), F32)], axis=0
        ).T
        ms.append(tall[:, 0:1] + tall[:, 1:2] + tall[:, 2:3])
        ls.append(tall[:, 3:4] + tall[:, 4:5] + tall[:, 5:6])
    return jnp.concatenate(ms, axis=0), jnp.concatenate(ls, axis=0)


def online(q, kv_ref, state, tile):
    m, l, o = state
    blocks, _, tokens, _ = kv_ref.shape
    for b in range(blocks):
        for t in range(0, tokens, tile):
            k = kv_ref[b, 0, t : t + tile, :]
            v = kv_ref[b, 1, t : t + tile, :]
            s = dot_t(q, k)
            top = jnp.max(s, axis=-1, keepdims=True)
            new = top if m is None else jnp.maximum(m, top)
            p = jnp.exp2(s * LOG2 - new * LOG2)
            pv = jnp.dot(
                p.astype(BF16),
                jnp.concatenate([v, jnp.ones_like(v)], axis=1),
                preferred_element_type=F32,
            )
            if m is None:
                l, o = pv[:, HD:], pv[:, :HD]
            else:
                fade = jnp.exp2((m - new) * LOG2)
                l, o = l * fade + pv[:, HD:], o * fade + pv[:, :HD]
            m = new
    return m, l, o


def first_kernel(q_ref, kv_ref, o_ref, st_ref, *, tile):
    m, l, o = online(q_ref[...], kv_ref, (None, None, None), tile)
    lane = lax.broadcasted_iota(jnp.int32, o.shape, 1)
    o_ref[...] = o
    st_ref[...] = jnp.where(lane < 64, jnp.broadcast_to(m, o.shape), l)


def second_kernel(q_ref, kv_ref, o_ref, st_ref, out_ref, *, tile):
    st = st_ref[...]
    m, l, o = online(q_ref[...], kv_ref, (st[:, 0:1], st[:, 64:65], o_ref[...]), tile)
    for i in range(q_ref.shape[0] // ROWS):
        rows = slice(i * ROWS, (i + 1) * ROWS)
        out_ref[i, :ROWS, :] = o[rows].astype(BF16)
        out_ref[i, ROWS:, :] = pack_stats(m[rows] * LOG2, l[rows, 0:1])


def prefix_first(q, kv, block, tile):
    n = q.shape[0]
    return pl.pallas_call(
        functools.partial(first_kernel, tile=tile),
        grid=(n // block,),
        in_specs=[
            pl.BlockSpec((block, HD), lambda i: (i, 0)),
            pl.BlockSpec(kv.shape, lambda i: (0, 0, 0, 0)),
        ],
        out_specs=[pl.BlockSpec((block, HD), lambda i: (i, 0))] * 2,
        out_shape=[jax.ShapeDtypeStruct((n, HD), F32)] * 2,
        compiler_params=pltpu.CompilerParams(vmem_limit_bytes=48 << 20),
        cost_estimate=pl.CostEstimate(
            flops=n * 2048 * HD * 4, bytes_accessed=8 << 20, transcendentals=n * 2048
        ),
        name="prefix_first",
    )(q, kv)


def prefix_second(q, kv, o, st, block, tile):
    n = q.shape[0]
    per = block // ROWS
    return pl.pallas_call(
        functools.partial(second_kernel, tile=tile),
        grid=(n // block,),
        in_specs=[
            pl.BlockSpec((block, HD), lambda i: (i, 0)),
            pl.BlockSpec(kv.shape, lambda i: (0, 0, 0, 0)),
            pl.BlockSpec((block, HD), lambda i: (i, 0)),
            pl.BlockSpec((block, HD), lambda i: (i, 0)),
        ],
        out_specs=pl.BlockSpec((per, PACK, HD), lambda i: (i, 0, 0)),
        out_shape=jax.ShapeDtypeStruct((n // ROWS, PACK, HD), BF16),
        compiler_params=pltpu.CompilerParams(vmem_limit_bytes=48 << 20),
        cost_estimate=pl.CostEstimate(
            flops=n * 2048 * HD * 4, bytes_accessed=8 << 20, transcendentals=n * 2048
        ),
        name="prefix_second",
    )(q, kv, o, st)


def softmax_part(s, v):
    m = jnp.maximum(jnp.max(s, axis=-1, keepdims=True), FLOOR)
    p = jnp.exp2(s * LOG2 - m * LOG2)
    l = jnp.sum(p, axis=-1, keepdims=True)
    o = jnp.dot(p.astype(BF16), v, preferred_element_type=F32)
    return m * LOG2, l, o


def page_kernel(slot_ref, req_ref, len_ref, q_ref, *rest):
    pages, out_ref = rest[:MAXP], rest[MAXP]
    t = pl.program_id(0)
    row = lax.broadcasted_iota(jnp.int32, (ROWS, PAGE), 0)
    token = lax.broadcasted_iota(jnp.int32, (ROWS, PAGE), 1)
    owner = lax.div(lax.rem(row, RS), STEPS)
    alive = jnp.concatenate(
        [
            (owner == req_ref[t * MAXP + c]) & (token < len_ref[t * MAXP + c])
            for c in range(MAXP)
        ],
        axis=1,
    )
    for k in range(KVH):
        cols = slice(k * HD, (k + 1) * HD)
        keys = jnp.concatenate([page[0, 0, :, cols] for page in pages], axis=0)
        vals = jnp.concatenate([page[0, 1, :, cols] for page in pages], axis=0)
        s = jnp.where(alive, dot_t(q_ref[0, k], keys), LOWEST)
        m, l, o = softmax_part(s, vals)
        out_ref[0, k, :ROWS, :] = o.astype(BF16)
        out_ref[0, k, ROWS:, :] = pack_stats(m, l)


def page_part(slots, reqs, lens, q, pool):
    n = q.shape[0]

    def page_spec(c):
        return pl.BlockSpec(
            (1, 2, PAGE, KVH * HD), lambda t, slot, req, size: (slot[t * MAXP + c], 0, 0, 0)
        )

    return pl.pallas_call(
        page_kernel,
        grid_spec=pltpu.PrefetchScalarGridSpec(
            num_scalar_prefetch=3,
            grid=(n,),
            in_specs=[pl.BlockSpec((1, KVH, ROWS, HD), lambda t, *_: (t, 0, 0, 0))]
            + [page_spec(c) for c in range(MAXP)],
            out_specs=pl.BlockSpec((1, KVH, PACK, HD), lambda t, *_: (t, 0, 0, 0)),
        ),
        out_shape=jax.ShapeDtypeStruct((n, KVH, PACK, HD), BF16),
        compiler_params=pltpu.CompilerParams(vmem_limit_bytes=48 << 20),
        cost_estimate=pl.CostEstimate(
            flops=n * KVH * ROWS * MAXP * PAGE * HD * 4,
            bytes_accessed=8 << 20,
            transcendentals=n * KVH * ROWS * MAXP * PAGE,
        ),
        name="page_part",
    )(slots, reqs, lens, q, *([pool] * MAXP))


def merge_kernel(q_ref, fresh_ref, part_ref, page_ref, out_ref):
    row = lax.broadcasted_iota(jnp.int32, (ROWS, RS), 0)
    col = lax.broadcasted_iota(jnp.int32, (ROWS, RS), 1)
    rs = lax.rem(row, RS)
    alive = (lax.div(rs, STEPS) == lax.div(col, STEPS)) & (
        lax.rem(col, STEPS) <= lax.rem(rs, STEPS)
    )
    s = jnp.where(alive, dot_t(q_ref[0], fresh_ref[0]), LOWEST)
    found = [softmax_part(s, fresh_ref[1])]
    for ref in (part_ref, page_ref):
        for i in range(ref.shape[0]):
            m, l = unpack_stats(ref[i, 0, ROWS:, :])
            found.append((m, l, ref[i, 0, :ROWS, :].astype(F32)))
    top = functools.reduce(jnp.maximum, [m for m, _, _ in found])
    weight_sum = jnp.zeros((ROWS, 1), F32)
    weighted = jnp.zeros((ROWS, HD), F32)
    for m, l, o in found:
        fade = jnp.exp2(m - top)
        weight_sum = weight_sum + l * fade
        weighted = weighted + o * fade
    result = (weighted / weight_sum).astype(BF16)
    for j in range(GQA):
        out_ref[:, j * HD : (j + 1) * HD] = result[j * RS : (j + 1) * RS]


def merge(q, fresh, parts, pages):
    return pl.pallas_call(
        merge_kernel,
        grid=(KVH,),
        in_specs=[
            pl.BlockSpec((1, ROWS, HD), lambda k: (k, 0, 0)),
            pl.BlockSpec((2, RS, HD), lambda k: (0, 0, k)),
            pl.BlockSpec((parts.shape[0], 1, PACK, HD), lambda k: (0, k, 0, 0)),
            pl.BlockSpec((pages.shape[0], 1, PACK, HD), lambda k: (0, k, 0, 0)),
        ],
        out_specs=pl.BlockSpec((RS, GQA * HD), lambda k: (0, k)),
        out_shape=jax.ShapeDtypeStruct((RS, HQ * HD), BF16),
        compiler_params=pltpu.CompilerParams(vmem_limit_bytes=48 << 20),
        name="merge",
    )(q, fresh, parts, pages)


def shift(x, axis, by):
    n = lax.axis_size(axis)
    return lax.ppermute(x, axis, [((i + by) % n, i) for i in range(n)])


def swap(x, axis, mask):
    return lax.ppermute(x, axis, [(i, i ^ mask) for i in range(lax.axis_size(axis))])


def page_places(unique_len, page_table):
    slot = jnp.arange(REQ * MAXP, dtype=jnp.int32)
    alive = jnp.clip(
        jnp.repeat(unique_len, MAXP) - (slot % MAXP) * PAGE, 0, PAGE
    )
    hit = page_table[0][:, None] == slot[None, :]
    req = jnp.sum(jnp.where(hit, (slot // MAXP)[:, None], 0), axis=0)
    size = jnp.sum(jnp.where(hit, alive[:, None], 0), axis=0)
    return jnp.stack([req, size])


def local(queries, prefix_kv, pool, new_kv, unique_len, page_table, send_slots):
    me = lax.axis_index("grp")
    q = queries.reshape(RS, KVH, GQA, HD).transpose(1, 2, 0, 3).reshape(KVH, ROWS, HD)

    places = page_places(unique_len, page_table).astype(BF16)
    places = jnp.pad(places, ((0, 14), (0, HD - REQ * MAXP)))
    asked = jnp.concatenate([q.reshape(KVH * ROWS, HD), places], axis=0)[None]
    asked = jnp.concatenate([asked, swap(asked, "grp", 2)], axis=0)
    asked = jnp.concatenate([asked, swap(asked, "grp", 1)], axis=0)
    rel = jnp.asarray([0, 2, 1, 3], jnp.int32)
    target = me ^ rel
    slots = send_slots[0].reshape(4, MAXP)[target].reshape(-1)
    info = asked[:, KVH * ROWS : KVH * ROWS + 2, : REQ * MAXP].reshape(4, 2, 4, MAXP)
    info = lax.dynamic_index_in_dim(info, me, 2, keepdims=False).astype(jnp.int32)
    q_all = asked[:, : KVH * ROWS].reshape(4, KVH, ROWS, HD)
    page_out = page_part(slots, info[:, 0].reshape(-1), info[:, 1].reshape(-1), q_all, pool)
    pages = jnp.stack(
        [page_out[0]] + [swap(page_out[i], "grp", g) for i, g in ((1, 2), (2, 1), (3, 3))]
    )

    kv = prefix_kv[0].reshape(-1, 2, KVH, HD).transpose(2, 1, 0, 3)
    tokens = kv.shape[2]
    sent = jnp.concatenate([q, kv.reshape(KVH, 2 * tokens, HD)], axis=1)
    came = lax.all_to_all(sent, "z", 0, 0, tiled=True)
    q_mine = came[:, :ROWS].reshape(4 * ROWS, HD)
    kv_mine = came[:, ROWS:].reshape(4, 2, tokens, HD)
    kv_other = swap(kv_mine, "xl", 1)
    copies = jnp.broadcast_to(q_mine[None], (4, 4 * ROWS, HD))
    q_rows = lax.all_to_all(copies, "y", 0, 0, tiled=True).reshape(16 * ROWS, HD)
    o, st = prefix_first(q_rows, kv_mine, 1024, 512)
    part = prefix_second(q_rows, kv_other, o, st, 1024, 512)
    part = lax.all_to_all(part, ("y", "z"), 0, 0, tiled=True)
    part = part.reshape(4, KVH, PACK, HD)

    fresh = new_kv.transpose(2, 0, 1, 3).reshape(2, RS, KVH * HD)
    result = merge(q, fresh, part, pages)
    return result.reshape(REQ, STEPS, HQ * HD)


def solution(mesh):
    fine = Mesh(mesh.devices.reshape(4, 4, 2, 4), AXES)
    every = P(AXES)
    dev = ("y", "xl", "z")
    placed = (every, P("grp", dev), every, every, every, every, every)
    return jax.shard_map(local, mesh=fine, in_specs=placed, out_specs=every, check_vma=False)
```

```python
import functools
import math

import jax
import jax.numpy as jnp
from jax import lax
from jax.experimental import pallas as pl
from jax.experimental.pallas import tpu as pltpu
from jax.sharding import Mesh, PartitionSpec as P

HQ = 64
KVH = 4
HD = 128
GQA = 16
STEPS = 4
PAGE = 128
MAXP = 6
REQ = 4
RS = REQ * STEPS
ROWS = RS * GQA
PACK = ROWS + 16
FLOOR = -1e29
LOWEST = -1e30
LOG2 = math.log2(math.e) / math.sqrt(HD)
AXES = ("grp", "y", "xl", "z")
F32 = jnp.float32
BF16 = jnp.bfloat16


def dot_t(a, b):
    return lax.dot_general(a, b, (((1,), (1,)), ((), ())), preferred_element_type=F32)


def split3(x):
    hi = x.astype(BF16).astype(F32)
    rest = x - hi
    mid = rest.astype(BF16).astype(F32)
    return hi, mid, rest - mid


def pack_stats(m, l):
    lane = lax.broadcasted_iota(jnp.int32, (128, 128), 1)
    row = lax.broadcasted_iota(jnp.int32, (8, 128), 0)
    parts = []
    for half in range(ROWS // 128):
        rows = slice(half * 128, half * 128 + 128)
        both = jnp.where(lane < 64, m[rows], l[rows]).T
        stats = jnp.zeros((8, 128), F32)
        for i, found in enumerate(split3(both[:8]) + split3(both[64:72])):
            stats = jnp.where(row == i, found, stats)
        parts.append(stats)
    return jnp.concatenate(parts, axis=0).astype(BF16)


def unpack_stats(packed, half):
    wide = packed.astype(F32)[half * 8 : half * 8 + 8]
    return wide[0:1] + wide[1:2] + wide[2:3], wide[3:4] + wide[4:5] + wide[5:6]


def widen(x, width):
    return jnp.concatenate([x] * (width // HD), axis=1)


def online(q, kv_ref, state, tile):
    m, l, o = state
    blocks, _, tokens, _ = kv_ref.shape
    for b in range(blocks):
        for t in range(0, tokens, tile):
            k = kv_ref[b, 0, t : t + tile, :]
            v = kv_ref[b, 1, t : t + tile, :]
            s = dot_t(q, k)
            top = jnp.broadcast_to(jnp.max(s, axis=-1, keepdims=True), (q.shape[0], HD))
            new = top if m is None else jnp.maximum(m, top)
            p = jnp.exp2(s * LOG2 - widen(new * LOG2, tile))
            pv = jnp.dot(
                p.astype(BF16),
                jnp.concatenate([v, jnp.ones_like(v)], axis=1),
                preferred_element_type=F32,
            )
            if m is None:
                l, o = pv[:, HD:], pv[:, :HD]
            else:
                fade = jnp.exp2((m - new) * LOG2)
                l, o = l * fade + pv[:, HD:], o * fade + pv[:, :HD]
            m = new
    return m, l, o


def first_kernel(q_ref, kv_ref, o_ref, m_ref, l_ref, *, tile):
    m_ref[...], l_ref[...], o_ref[...] = online(q_ref[...], kv_ref, (None, None, None), tile)


def second_kernel(q_ref, kv_ref, o_ref, m_ref, l_ref, out_ref, *, tile):
    m, l, o = online(q_ref[...], kv_ref, (m_ref[...], l_ref[...], o_ref[...]), tile)
    for i in range(q_ref.shape[0] // ROWS):
        rows = slice(i * ROWS, (i + 1) * ROWS)
        out_ref[i, :ROWS, :] = o[rows].astype(BF16)
        out_ref[i, ROWS:, :] = pack_stats(m[rows] * LOG2, l[rows])


def prefix_cost(n):
    return pl.CostEstimate(
        flops=n * 2048 * HD * 16, bytes_accessed=16 << 20, transcendentals=n * 2048
    )


def prefix_first(q, kv, block, tile):
    n = q.shape[0]
    rows = pl.BlockSpec((block, HD), lambda i: (i, 0))
    return pl.pallas_call(
        functools.partial(first_kernel, tile=tile),
        grid=(n // block,),
        in_specs=[rows, pl.BlockSpec(kv.shape, lambda i: (0, 0, 0, 0))],
        out_specs=[rows] * 3,
        out_shape=[jax.ShapeDtypeStruct((n, HD), F32)] * 3,
        compiler_params=pltpu.CompilerParams(vmem_limit_bytes=48 << 20),
        cost_estimate=prefix_cost(n),
        name="prefix_first",
    )(q, kv)


def prefix_second(q, kv, state, block, tile):
    n = q.shape[0]
    per = block // ROWS
    rows = pl.BlockSpec((block, HD), lambda i: (i, 0))
    return pl.pallas_call(
        functools.partial(second_kernel, tile=tile),
        grid=(n // block,),
        in_specs=[rows, pl.BlockSpec(kv.shape, lambda i: (0, 0, 0, 0)), rows, rows, rows],
        out_specs=pl.BlockSpec((per, PACK, HD), lambda i: (i, 0, 0)),
        out_shape=jax.ShapeDtypeStruct((n // ROWS, PACK, HD), BF16),
        compiler_params=pltpu.CompilerParams(vmem_limit_bytes=48 << 20),
        cost_estimate=prefix_cost(n),
        name="prefix_second",
    )(q, kv, *state)


def page_kernel(slot_ref, req_ref, len_ref, q_ref, fresh_ref, *rest):
    pages, out_ref = rest[:MAXP], rest[MAXP]
    t = pl.program_id(0)
    row = lax.broadcasted_iota(jnp.int32, (ROWS, PAGE), 0)
    token = lax.broadcasted_iota(jnp.int32, (ROWS, PAGE), 1)
    step = lax.rem(row, RS)
    owner = lax.div(step, STEPS)
    bounds = [
        jnp.where(owner == req_ref[t * MAXP + c], len_ref[t * MAXP + c], 0) for c in range(MAXP)
    ]

    def attend(own):
        for k in range(KVH):
            cols = slice(k * HD, (k + 1) * HD)
            keys = [page[0, 0, :, cols] for page in pages]
            vals = [page[0, 1, :, cols] for page in pages]
            if own:
                keys.append(fresh_ref[0, :, cols])
                vals.append(fresh_ref[1, :, cols])
            s = dot_t(q_ref[0, k], jnp.concatenate(keys, axis=0))
            parts = [
                jnp.where(token < bounds[c], s[:, c * PAGE : (c + 1) * PAGE], LOWEST)
                for c in range(MAXP)
            ]
            if own:
                alive = (
                    (lax.div(token, STEPS) == owner)
                    & (lax.rem(token, STEPS) <= lax.rem(step, STEPS))
                    & (token < RS)
                )
                parts.append(jnp.where(alive, s[:, MAXP * PAGE :], LOWEST))
            top = jnp.max(functools.reduce(jnp.maximum, parts), axis=-1, keepdims=True)
            m = jnp.maximum(jnp.broadcast_to(top, (ROWS, HD)), FLOOR) * LOG2
            p = [jnp.exp2(part * LOG2 - m).astype(BF16) for part in parts]
            v = jnp.concatenate(vals, axis=0)
            pv = jnp.dot(
                jnp.concatenate(p, axis=1),
                jnp.concatenate([v, jnp.ones_like(v)], axis=1),
                preferred_element_type=F32,
            )
            out_ref[0, k, :ROWS, :] = pv[:, :HD].astype(BF16)
            out_ref[0, k, ROWS:, :] = pack_stats(m, pv[:, HD:])

    @pl.when(t == 0)
    def _():
        attend(True)

    @pl.when(t != 0)
    def _():
        attend(False)


def page_part(slots, reqs, lens, q, fresh, pool):
    n = q.shape[0]

    def page_spec(c):
        return pl.BlockSpec(
            (1, 2, PAGE, KVH * HD), lambda t, slot, req, size: (slot[t * MAXP + c], 0, 0, 0)
        )

    return pl.pallas_call(
        page_kernel,
        grid_spec=pltpu.PrefetchScalarGridSpec(
            num_scalar_prefetch=3,
            grid=(n,),
            in_specs=[
                pl.BlockSpec((1, KVH, ROWS, HD), lambda t, *_: (t, 0, 0, 0)),
                pl.BlockSpec(fresh.shape, lambda t, *_: (0, 0, 0)),
            ]
            + [page_spec(c) for c in range(MAXP)],
            out_specs=pl.BlockSpec((1, KVH, PACK, HD), lambda t, *_: (t, 0, 0, 0)),
        ),
        out_shape=jax.ShapeDtypeStruct((n, KVH, PACK, HD), BF16),
        compiler_params=pltpu.CompilerParams(vmem_limit_bytes=48 << 20),
        cost_estimate=pl.CostEstimate(
            flops=n * KVH * ROWS * MAXP * PAGE * HD * 16,
            bytes_accessed=8 << 20,
            transcendentals=n * KVH * ROWS * MAXP * PAGE,
        ),
        name="page_part",
    )(slots, reqs, lens, q, fresh, *([pool] * MAXP))


def merge_kernel(part_ref, *rest):
    page_refs, out_ref = rest[:-1], rest[-1]
    found = [part_ref.at[i, 0] for i in range(part_ref.shape[0])]
    found += [ref.at[0] for ref in page_refs]
    for half in range(ROWS // 128):
        stats = [unpack_stats(ref[ROWS:, :], half) for ref in found]
        top = functools.reduce(jnp.maximum, [m for m, _ in stats])
        fades = [jnp.exp2(m - top) for m, _ in stats]
        weight_sum = functools.reduce(jnp.add, [l * f for (_, l), f in zip(stats, fades)])
        gains = jnp.concatenate(
            [f / weight_sum for f in fades] + [jnp.zeros((128 - len(fades), 128), F32)], axis=0
        ).T
        total = jnp.zeros((128, HD), F32)
        for i, ref in enumerate(found):
            gain = jnp.broadcast_to(gains[:, i : i + 1], (128, HD))
            total = total + ref[half * 128 : half * 128 + 128, :].astype(F32) * gain
        total = total.astype(BF16)
        for j in range(128 // RS):
            col = half * 128 // RS + j
            out_ref[:, col * HD : (col + 1) * HD] = total[j * RS : (j + 1) * RS]


def merge(parts, pages):
    return pl.pallas_call(
        merge_kernel,
        grid=(KVH,),
        in_specs=[pl.BlockSpec((parts.shape[0], 1, PACK, HD), lambda k: (0, k, 0, 0))]
        + [pl.BlockSpec((1, PACK, HD), lambda k: (k, 0, 0))] * len(pages),
        out_specs=pl.BlockSpec((RS, GQA * HD), lambda k: (0, k)),
        out_shape=jax.ShapeDtypeStruct((RS, HQ * HD), BF16),
        compiler_params=pltpu.CompilerParams(vmem_limit_bytes=48 << 20),
        name="merge",
    )(parts, *pages)


def swap(x, axis, mask):
    return lax.ppermute(x, axis, [(i, i ^ mask) for i in range(lax.axis_size(axis))])


def page_places(unique_len, page_table):
    slot = jnp.arange(REQ * MAXP, dtype=jnp.int32)
    alive = jnp.clip(
        jnp.repeat(unique_len, MAXP) - (slot % MAXP) * PAGE, 0, PAGE
    )
    hit = page_table[0][:, None] == slot[None, :]
    req = jnp.sum(jnp.where(hit, (slot // MAXP)[:, None], 0), axis=0)
    size = jnp.sum(jnp.where(hit, alive[:, None], 0), axis=0)
    return jnp.stack([req, size])


def after(x, *done):
    return lax.optimization_barrier((x, *done))[0]


def local(queries, prefix_kv, pool, new_kv, unique_len, page_table, send_slots):
    me = lax.axis_index("grp")
    kv = prefix_kv[0].reshape(-1, 2, KVH, HD).transpose(2, 1, 0, 3)
    tokens = kv.shape[2]
    kv_near = swap(kv, "xl", 1)
    kv_mine = lax.all_to_all(kv, "z", 0, 0, tiled=True)

    q = queries.reshape(RS, KVH, GQA, HD).transpose(1, 2, 0, 3).reshape(KVH, ROWS, HD)
    copies = jnp.broadcast_to(q[None], (4, KVH, ROWS, HD)).reshape(4 * KVH, ROWS, HD)
    q_rows = lax.all_to_all(copies, ("y", "z"), 0, 0, tiled=True).reshape(16 * ROWS, HD)

    places = page_places(unique_len, page_table).astype(BF16)
    places = jnp.pad(places, ((0, 14), (0, HD - REQ * MAXP)))
    asked = jnp.concatenate([q.reshape(KVH * ROWS, HD), places], axis=0)[None]
    asked = jnp.concatenate([asked, swap(asked, "grp", 2)], axis=0)
    asked = jnp.concatenate([asked, swap(asked, "grp", 1)], axis=0)
    rel = jnp.asarray([0, 2, 1, 3], jnp.int32)
    target = me ^ rel
    slots = send_slots[0].reshape(4, MAXP)[target].reshape(-1)
    info = asked[:, KVH * ROWS : KVH * ROWS + 2, : REQ * MAXP].reshape(4, 2, 4, MAXP)
    info = lax.dynamic_index_in_dim(info, me, 2, keepdims=False).astype(jnp.int32)
    q_all = asked[:, : KVH * ROWS].reshape(4, KVH, ROWS, HD)
    fresh = new_kv.transpose(2, 0, 1, 3).reshape(2, RS, KVH * HD)
    fresh = jnp.pad(fresh, ((0, 0), (0, PAGE - RS), (0, 0)))
    page_out = page_part(
        slots, info[:, 0].reshape(-1), info[:, 1].reshape(-1), q_all, fresh, pool
    )

    kv_other = lax.all_to_all(kv_near, "z", 0, 0, tiled=True)
    q_rows = after(q_rows, page_out)
    state = prefix_first(q_rows, kv_mine, 1024, 256)
    pages = [page_out[0]] + [swap(page_out[i], "grp", g) for i, g in ((1, 2), (2, 1), (3, 3))]
    part = prefix_second(q_rows, kv_other, state, 1024, 256)
    part = lax.all_to_all(part, ("y", "z"), 0, 0, tiled=True)
    part = part.reshape(4, KVH, PACK, HD)
    return merge(part, pages).reshape(REQ, STEPS, HQ * HD)


def solution(mesh):
    fine = Mesh(mesh.devices.reshape(4, 4, 2, 4), AXES)
    every = P(AXES)
    dev = ("y", "xl", "z")
    placed = (every, P("grp", dev), every, every, every, every, every)
    return jax.shard_map(local, mesh=fine, in_specs=placed, out_specs=every, check_vma=False)
```

```python
import functools
import math

import jax
import jax.numpy as jnp
from jax import lax
from jax.experimental import pallas as pl
from jax.experimental.pallas import tpu as pltpu
from jax.sharding import Mesh, PartitionSpec as P

HQ = 64
KVH = 4
HD = 128
GQA = 16
STEPS = 4
PAGE = 128
MAXP = 6
REQ = 4
RS = REQ * STEPS
ROWS = RS * GQA
PACK = ROWS + 16
FLOOR = -1e29
LOWEST = -1e30
LOG2 = math.log2(math.e) / math.sqrt(HD)
AXES = ("grp", "y", "xl", "z")
F32 = jnp.float32
BF16 = jnp.bfloat16


def dot_t(a, b):
    return lax.dot_general(a, b, (((1,), (1,)), ((), ())), preferred_element_type=F32)


def split3(x):
    hi = x.astype(BF16).astype(F32)
    rest = x - hi
    mid = rest.astype(BF16).astype(F32)
    return hi, mid, rest - mid


def pack_stats(m, l):
    lane = lax.broadcasted_iota(jnp.int32, (128, 128), 1)
    row = lax.broadcasted_iota(jnp.int32, (8, 128), 0)
    parts = []
    for half in range(ROWS // 128):
        rows = slice(half * 128, half * 128 + 128)
        both = jnp.where(lane < 64, m[rows], l[rows]).T
        stats = jnp.zeros((8, 128), F32)
        for i, found in enumerate(split3(both[:8]) + split3(both[64:72])):
            stats = jnp.where(row == i, found, stats)
        parts.append(stats)
    return jnp.concatenate(parts, axis=0).astype(BF16)


def unpack_stats(packed, half):
    wide = packed.astype(F32)[half * 8 : half * 8 + 8]
    return wide[0:1] + wide[1:2] + wide[2:3], wide[3:4] + wide[4:5] + wide[5:6]


def widen(x, width):
    return jnp.concatenate([x] * (width // HD), axis=1)


def online(q, kv_ref, state, tile):
    m, l, o = state
    blocks, _, tokens, _ = kv_ref.shape
    for b in range(blocks):
        for t in range(0, tokens, tile):
            k = kv_ref[b, 0, t : t + tile, :]
            v = kv_ref[b, 1, t : t + tile, :]
            s = dot_t(q, k)
            top = jnp.broadcast_to(jnp.max(s, axis=-1, keepdims=True), (q.shape[0], HD))
            new = top if m is None else jnp.maximum(m, top)
            p = jnp.exp2(s * LOG2 - widen(new * LOG2, tile))
            pv = jnp.dot(
                p.astype(BF16),
                jnp.concatenate([v, jnp.ones_like(v)], axis=1),
                preferred_element_type=F32,
            )
            if m is None:
                l, o = pv[:, HD:], pv[:, :HD]
            else:
                fade = jnp.exp2((m - new) * LOG2)
                l, o = l * fade + pv[:, HD:], o * fade + pv[:, :HD]
            m = new
    return m, l, o


def prefix_kernel(at_ref, *refs, tile):
    q_refs, kv_ref, out_ref, held = refs[:4], refs[4], refs[5], refs[6]
    i = pl.program_id(0)

    @pl.when(i == 0)
    def _():
        for n, q_ref in enumerate(q_refs):
            held[n] = q_ref[...]

    m, l, o = online(held[i], kv_ref, (None, None, None), tile)
    for n in range(4):
        rows = slice(n * ROWS, (n + 1) * ROWS)
        place = lax.rem(at_ref[1] + n, 4)
        out_ref[place, :ROWS, :] = o[rows].astype(BF16)
        out_ref[place, ROWS:, :] = pack_stats(m[rows] * LOG2, l[rows])


def prefix_part(at, qs, kv, tile):
    rows = qs[0].shape[0]
    tokens = kv.shape[0] * kv.shape[2]
    return pl.pallas_call(
        functools.partial(prefix_kernel, tile=tile),
        grid_spec=pltpu.PrefetchScalarGridSpec(
            num_scalar_prefetch=1,
            grid=(4,),
            in_specs=[pl.BlockSpec((rows, HD), lambda i, at: (0, 0))] * 4
            + [pl.BlockSpec(kv.shape, lambda i, at: (0, 0, 0, 0))],
            out_specs=pl.BlockSpec((4, PACK, HD), lambda i, at: (lax.rem(at[0] + i, 4), 0, 0)),
            scratch_shapes=[pltpu.VMEM((4, rows, HD), BF16)],
        ),
        out_shape=jax.ShapeDtypeStruct((16, PACK, HD), BF16),
        compiler_params=pltpu.CompilerParams(vmem_limit_bytes=48 << 20),
        cost_estimate=pl.CostEstimate(
            flops=rows * tokens * HD * 32,
            bytes_accessed=8 << 20,
            transcendentals=4 * rows * tokens,
        ),
        name="prefix_part",
    )(at, *qs, kv)


def page_kernel(slot_ref, req_ref, len_ref, q_ref, fresh_ref, *rest):
    pages, out_ref = rest[:MAXP], rest[MAXP]
    t = pl.program_id(0)
    row = lax.broadcasted_iota(jnp.int32, (ROWS, PAGE), 0)
    token = lax.broadcasted_iota(jnp.int32, (ROWS, PAGE), 1)
    step = lax.rem(row, RS)
    owner = lax.div(step, STEPS)
    bounds = [
        jnp.where(owner == req_ref[t * MAXP + c], len_ref[t * MAXP + c], 0) for c in range(MAXP)
    ]

    def attend(own):
        for k in range(KVH):
            cols = slice(k * HD, (k + 1) * HD)
            keys = [page[0, 0, :, cols] for page in pages]
            vals = [page[0, 1, :, cols] for page in pages]
            if own:
                keys.append(fresh_ref[0, :, cols])
                vals.append(fresh_ref[1, :, cols])
            s = dot_t(q_ref[0, k], jnp.concatenate(keys, axis=0))
            parts = [
                jnp.where(token < bounds[c], s[:, c * PAGE : (c + 1) * PAGE], LOWEST)
                for c in range(MAXP)
            ]
            if own:
                alive = (
                    (lax.div(token, STEPS) == owner)
                    & (lax.rem(token, STEPS) <= lax.rem(step, STEPS))
                    & (token < RS)
                )
                parts.append(jnp.where(alive, s[:, MAXP * PAGE :], LOWEST))
            top = jnp.max(functools.reduce(jnp.maximum, parts), axis=-1, keepdims=True)
            m = jnp.maximum(jnp.broadcast_to(top, (ROWS, HD)), FLOOR) * LOG2
            p = [jnp.exp2(part * LOG2 - m).astype(BF16) for part in parts]
            v = jnp.concatenate(vals, axis=0)
            pv = jnp.dot(
                jnp.concatenate(p, axis=1),
                jnp.concatenate([v, jnp.ones_like(v)], axis=1),
                preferred_element_type=F32,
            )
            out_ref[0, k, :ROWS, :] = pv[:, :HD].astype(BF16)
            out_ref[0, k, ROWS:, :] = pack_stats(m, pv[:, HD:])

    @pl.when(t == 0)
    def _():
        attend(True)

    @pl.when(t != 0)
    def _():
        attend(False)


def page_part(slots, reqs, lens, q, fresh, pool):
    n = q.shape[0]

    def page_spec(c):
        return pl.BlockSpec(
            (1, 2, PAGE, KVH * HD), lambda t, slot, req, size: (slot[t * MAXP + c], 0, 0, 0)
        )

    return pl.pallas_call(
        page_kernel,
        grid_spec=pltpu.PrefetchScalarGridSpec(
            num_scalar_prefetch=3,
            grid=(n,),
            in_specs=[
                pl.BlockSpec((1, KVH, ROWS, HD), lambda t, *_: (t, 0, 0, 0)),
                pl.BlockSpec(fresh.shape, lambda t, *_: (0, 0, 0)),
            ]
            + [page_spec(c) for c in range(MAXP)],
            out_specs=pl.BlockSpec((1, KVH, PACK, HD), lambda t, *_: (t, 0, 0, 0)),
        ),
        out_shape=jax.ShapeDtypeStruct((n, KVH, PACK, HD), BF16),
        compiler_params=pltpu.CompilerParams(vmem_limit_bytes=48 << 20),
        cost_estimate=pl.CostEstimate(
            flops=n * KVH * ROWS * MAXP * PAGE * HD * 16,
            bytes_accessed=8 << 20,
            transcendentals=n * KVH * ROWS * MAXP * PAGE,
        ),
        name="page_part",
    )(slots, reqs, lens, q, fresh, *([pool] * MAXP))


def merge_kernel(part_ref, *rest):
    page_refs, out_ref = rest[:-1], rest[-1]
    found = [part_ref.at[i, 0] for i in range(part_ref.shape[0])]
    found += [ref.at[0] for ref in page_refs]
    for half in range(ROWS // 128):
        stats = [unpack_stats(ref[ROWS:, :], half) for ref in found]
        top = functools.reduce(jnp.maximum, [m for m, _ in stats])
        fades = [jnp.exp2(m - top) for m, _ in stats]
        weight_sum = functools.reduce(jnp.add, [l * f for (_, l), f in zip(stats, fades)])
        gains = jnp.concatenate(
            [f / weight_sum for f in fades] + [jnp.zeros((128 - len(fades), 128), F32)], axis=0
        ).T
        total = jnp.zeros((128, HD), F32)
        for i, ref in enumerate(found):
            gain = jnp.broadcast_to(gains[:, i : i + 1], (128, HD))
            total = total + ref[half * 128 : half * 128 + 128, :].astype(F32) * gain
        total = total.astype(BF16)
        for j in range(128 // RS):
            col = half * 128 // RS + j
            out_ref[:, col * HD : (col + 1) * HD] = total[j * RS : (j + 1) * RS]


def merge(parts, pages):
    return pl.pallas_call(
        merge_kernel,
        grid=(KVH,),
        in_specs=[pl.BlockSpec((parts.shape[0], 1, PACK, HD), lambda k: (0, k, 0, 0))]
        + [pl.BlockSpec((1, PACK, HD), lambda k: (k, 0, 0))] * len(pages),
        out_specs=pl.BlockSpec((RS, GQA * HD), lambda k: (0, k)),
        out_shape=jax.ShapeDtypeStruct((RS, HQ * HD), BF16),
        compiler_params=pltpu.CompilerParams(vmem_limit_bytes=48 << 20),
        name="merge",
    )(parts, *pages)


def swap(x, axis, mask):
    return lax.ppermute(x, axis, [(i, i ^ mask) for i in range(lax.axis_size(axis))])


def fetch(x, axis, by):
    n = lax.axis_size(axis)
    return lax.ppermute(x, axis, [((i + by) % n, i) for i in range(n)])


def page_places(unique_len, page_table):
    slot = jnp.arange(REQ * MAXP, dtype=jnp.int32)
    alive = jnp.clip(
        jnp.repeat(unique_len, MAXP) - (slot % MAXP) * PAGE, 0, PAGE
    )
    hit = page_table[0][:, None] == slot[None, :]
    req = jnp.sum(jnp.where(hit, (slot // MAXP)[:, None], 0), axis=0)
    size = jnp.sum(jnp.where(hit, alive[:, None], 0), axis=0)
    return jnp.stack([req, size])


def after(x, *done):
    return lax.optimization_barrier((x, *done))[0]


def local(queries, prefix_kv, pool, new_kv, unique_len, page_table, send_slots):
    me, y, z = (lax.axis_index(name) for name in ("grp", "y", "z"))
    kv = prefix_kv[0].reshape(-1, 2, KVH, HD).transpose(2, 1, 0, 3)
    tokens = kv.shape[2]
    kv = jnp.broadcast_to(kv[None], (2, *kv.shape)).reshape(8, 2, tokens, HD)
    kv_all = lax.all_to_all(kv, ("xl", "z"), 0, 0, tiled=True)

    q = after(queries, kv).reshape(RS, KVH, GQA, HD).transpose(1, 2, 0, 3).reshape(KVH, ROWS, HD)

    def head_of(by):
        return lax.dynamic_index_in_dim(q, lax.rem(z + 4 - by, 4), 0, keepdims=False)

    rows = jnp.concatenate([head_of(0)] + [fetch(head_of(k), "z", k) for k in (1, 2, 3)], axis=0)
    qs = [rows] + [fetch(rows, "y", k) for k in (1, 2, 3)]

    places = page_places(unique_len, page_table).astype(BF16)
    places = jnp.pad(places, ((0, 14), (0, HD - REQ * MAXP)))
    asked = jnp.concatenate([q.reshape(KVH * ROWS, HD), places], axis=0)[None]
    asked = jnp.concatenate([asked, swap(asked, "grp", 2)], axis=0)
    asked = jnp.concatenate([asked, swap(asked, "grp", 1)], axis=0)
    rel = jnp.asarray([0, 2, 1, 3], jnp.int32)
    target = me ^ rel
    slots = send_slots[0].reshape(4, MAXP)[target].reshape(-1)
    info = asked[:, KVH * ROWS : KVH * ROWS + 2, : REQ * MAXP].reshape(4, 2, 4, MAXP)
    info = lax.dynamic_index_in_dim(info, me, 2, keepdims=False).astype(jnp.int32)
    q_all = asked[:, : KVH * ROWS].reshape(4, KVH, ROWS, HD)
    fresh = new_kv.transpose(2, 0, 1, 3).reshape(2, RS, KVH * HD)
    fresh = jnp.pad(fresh, ((0, 0), (0, PAGE - RS), (0, 0)))
    page_out = page_part(
        slots, info[:, 0].reshape(-1), info[:, 1].reshape(-1), q_all, fresh, pool
    )

    at = after(jnp.stack([y, z]), page_out)
    part = prefix_part(at, qs, kv_all, 256)
    pages = [page_out[0]] + [swap(page_out[i], "grp", g) for i, g in ((1, 2), (2, 1), (3, 3))]
    part = lax.all_to_all(part, ("y", "z"), 0, 0, tiled=True)
    part = part.reshape(4, KVH, PACK, HD)
    return merge(part, pages).reshape(REQ, STEPS, HQ * HD)


def solution(mesh):
    fine = Mesh(mesh.devices.reshape(4, 4, 2, 4), AXES)
    every = P(AXES)
    dev = ("y", "xl", "z")
    placed = (every, P("grp", dev), every, every, every, every, every)
    return jax.shard_map(local, mesh=fine, in_specs=placed, out_specs=every, check_vma=False)
```

```python
import functools
import math

import jax
import jax.numpy as jnp
from jax import lax
from jax.experimental import pallas as pl
from jax.experimental.pallas import tpu as pltpu
from jax.sharding import Mesh, PartitionSpec as P

HQ = 64
KVH = 4
HD = 128
GQA = 16
STEPS = 4
PAGE = 128
MAXP = 6
REQ = 4
RS = REQ * STEPS
ROWS = RS * GQA
PACK = ROWS + 16
FLOOR = -1e29
LOWEST = -1e30
LOG2 = math.log2(math.e) / math.sqrt(HD)
AXES = ("grp", "y", "xl", "z")
F32 = jnp.float32
BF16 = jnp.bfloat16


def dot_t(a, b):
    return lax.dot_general(a, b, (((1,), (1,)), ((), ())), preferred_element_type=F32)


def split3(x):
    hi = x.astype(BF16).astype(F32)
    rest = x - hi
    mid = rest.astype(BF16).astype(F32)
    return hi, mid, rest - mid


def pack_stats(m, l):
    lane = lax.broadcasted_iota(jnp.int32, (128, 128), 1)
    row = lax.broadcasted_iota(jnp.int32, (8, 128), 0)
    parts = []
    for half in range(ROWS // 128):
        rows = slice(half * 128, half * 128 + 128)
        both = jnp.where(lane < 64, m[rows], l[rows]).T
        stats = jnp.zeros((8, 128), F32)
        for i, found in enumerate(split3(both[:8]) + split3(both[64:72])):
            stats = jnp.where(row == i, found, stats)
        parts.append(stats)
    return jnp.concatenate(parts, axis=0).astype(BF16)


def unpack_stats(packed, half):
    wide = packed.astype(F32)[half * 8 : half * 8 + 8]
    return wide[0:1] + wide[1:2] + wide[2:3], wide[3:4] + wide[4:5] + wide[5:6]


def widen(x, width):
    return jnp.concatenate([x] * (width // HD), axis=1)


def scaled(q):
    wide = q.astype(F32) * LOG2
    high = wide.astype(BF16)
    return jnp.concatenate([high, (wide - high.astype(F32)).astype(BF16)], axis=1)


def online(q, kv_ref, tile):
    m = l = o = None
    q = scaled(q)
    blocks, _, tokens, _ = kv_ref.shape
    for b in range(blocks):
        for t in range(0, tokens, tile):
            k = kv_ref[b, 0, t : t + tile, :]
            v = kv_ref[b, 1, t : t + tile, :]
            s = dot_t(q, jnp.concatenate([k, k], axis=1))
            top = jnp.broadcast_to(jnp.max(s, axis=-1, keepdims=True), (q.shape[0], HD))
            new = top if m is None else jnp.maximum(m, top)
            p = jnp.exp2(s - widen(new, tile))
            pv = jnp.dot(
                p.astype(BF16),
                jnp.concatenate([v, jnp.ones_like(v)], axis=1),
                preferred_element_type=F32,
            )
            if m is None:
                l, o = pv[:, HD:], pv[:, :HD]
            else:
                fade = jnp.exp2(m - new)
                l, o = l * fade + pv[:, HD:], o * fade + pv[:, :HD]
            m = new
    return m, l, o


def prefix_kernel(at_ref, *refs, count, tile):
    q_refs, kv_ref, out_ref, held = refs[:count], refs[count], refs[-2], refs[-1]
    i = pl.program_id(0)

    @pl.when(i == 0)
    def _():
        for n, q_ref in enumerate(q_refs):
            held[n] = q_ref[...].reshape(4 * ROWS, HD)

    m, l, o = online(held[i], kv_ref, tile)
    for n in range(4):
        part = slice(n * ROWS, (n + 1) * ROWS)
        place = lax.rem(at_ref[0] + n, 4)
        out_ref[place, :ROWS, :] = o[part].astype(BF16)
        out_ref[place, ROWS:, :] = pack_stats(m[part], l[part])


def prefix_part(at, qs, kv, first, done, tile):
    count = len(qs)
    tokens = kv.shape[0] * kv.shape[2]
    return pl.pallas_call(
        functools.partial(prefix_kernel, count=count, tile=tile),
        grid_spec=pltpu.PrefetchScalarGridSpec(
            num_scalar_prefetch=1,
            grid=(count,),
            in_specs=[pl.BlockSpec(qs[0].shape, lambda i, at: (0, 0, 0))] * count
            + [pl.BlockSpec(kv.shape, lambda i, at: (0, 0, 0, 0))]
            + [pl.BlockSpec(memory_space=pl.ANY)] * len(done),
            out_specs=pl.BlockSpec(
                (4, PACK, HD), lambda i, at: (lax.rem(at[1] + i + first, 4), 0, 0)
            ),
            scratch_shapes=[pltpu.VMEM((count, 4 * ROWS, HD), BF16)],
        ),
        out_shape=jax.ShapeDtypeStruct((16, PACK, HD), BF16),
        input_output_aliases={count + 2: 0} if done else {},
        compiler_params=pltpu.CompilerParams(vmem_limit_bytes=40 << 20),
        cost_estimate=pl.CostEstimate(
            flops=count * ROWS * tokens * HD * 32,
            bytes_accessed=8 << 20,
            transcendentals=count * ROWS * tokens * 4,
        ),
        name="prefix_part",
    )(at, *qs, kv, *done)


def prep_kernel(table_ref, size_ref, q_ref, kv_ref, asked_ref, dealt_ref):
    for c in range(GQA):
        tile = q_ref[:, :, c * HD : (c + 1) * HD].reshape(RS, HD)
        asked_ref[0, c * RS : (c + 1) * RS, :] = tile
    both = kv_ref[0].astype(F32)
    for i in range(2):
        half = both[:, i].astype(BF16)
        dealt_ref[0, 0, i] = half
        dealt_ref[1, 0, i] = half

    @pl.when(pl.program_id(0) == 0)
    def _():
        lane = lax.broadcasted_iota(jnp.int32, (16, HD), 1)
        row = lax.broadcasted_iota(jnp.int32, (16, HD), 0)
        notes = jnp.zeros((16, HD), jnp.int32)
        for slot in range(REQ * MAXP):
            req, page = divmod(slot, MAXP)
            alive = jnp.clip(size_ref[0:1, req : req + 1] - page * PAGE, 0, PAGE)
            here = jnp.where(row == 0, req, jnp.where(row == 1, alive, 0))
            notes = jnp.where(lane == table_ref[0:1, slot : slot + 1], here, notes)
        asked_ref[0, ROWS:, :] = notes.astype(F32).astype(BF16)

    @pl.when(pl.program_id(0) != 0)
    def _():
        asked_ref[0, ROWS:, :] = jnp.zeros((16, HD), BF16)


def prep(page_table, unique_len, queries, prefix_kv):
    tokens = prefix_kv.shape[1]
    return pl.pallas_call(
        prep_kernel,
        grid=(KVH,),
        in_specs=[
            pl.BlockSpec(page_table.shape, lambda k: (0, 0)),
            pl.BlockSpec((1, REQ), lambda k: (0, 0)),
            pl.BlockSpec((REQ, STEPS, GQA * HD), lambda k: (0, 0, k)),
            pl.BlockSpec((1, tokens, 2, HD), lambda k: (0, 0, 0, k)),
        ],
        out_specs=[
            pl.BlockSpec((1, PACK, HD), lambda k: (k, 0, 0)),
            pl.BlockSpec((2, 1, 2, tokens, HD), lambda k: (0, k, 0, 0, 0)),
        ],
        out_shape=[
            jax.ShapeDtypeStruct((KVH, PACK, HD), BF16),
            jax.ShapeDtypeStruct((2, KVH, 2, tokens, HD), BF16),
        ],
        compiler_params=pltpu.CompilerParams(vmem_limit_bytes=60 << 20),
        name="prep",
    )(page_table, unique_len.reshape(1, REQ), queries, prefix_kv)


def pick_kernel(at_ref, *refs):
    q_refs, out_refs = refs[:4], refs[4:]
    for k, out_ref in enumerate(out_refs):
        head = lax.rem(at_ref[1] + 4 - k, 4)
        for n, q_ref in enumerate(q_refs):
            out_ref[n] = q_ref[head, :ROWS, :]


def pick(at, asked):
    scalar = pl.BlockSpec(memory_space=pltpu.SMEM)
    whole = pl.BlockSpec(memory_space=pltpu.VMEM)
    return pl.pallas_call(
        pick_kernel,
        in_specs=[scalar] + [whole] * 4,
        out_specs=[whole] * 4,
        out_shape=[jax.ShapeDtypeStruct((4, ROWS, HD), BF16)] * 4,
        compiler_params=pltpu.CompilerParams(vmem_limit_bytes=32 << 20),
        name="pick",
    )(at, *asked)


def page_kernel(at_ref, slot_ref, *refs, first):
    q_refs, fresh_ref, pages = refs[:2], refs[2], refs[3 : 3 + MAXP]
    out_refs, (held, found) = refs[3 + MAXP : 5 + MAXP], refs[5 + MAXP :]
    t = pl.program_id(0)

    @pl.when(t == 0)
    def _():
        for n, q_ref in enumerate(q_refs):
            held[n] = q_ref[...]

    row = lax.broadcasted_iota(jnp.int32, (ROWS, PAGE), 0)
    token = lax.broadcasted_iota(jnp.int32, (ROWS, PAGE), 1)
    step = lax.rem(row, RS)
    owner = lax.div(step, STEPS)
    notes = held[t, 0, ROWS:, :].astype(F32)
    place = lax.broadcasted_iota(jnp.int32, (1, HD), 1)
    bounds = []
    for c in range(MAXP):
        here = place == at_ref[2] * MAXP + c
        req, size = (
            jnp.sum(jnp.where(here, notes[i : i + 1], 0.0), axis=1, keepdims=True).astype(jnp.int32)
            for i in range(2)
        )
        bounds.append(jnp.where(owner == req, size, 0))

    def attend(own):
        scores, vals = [], []
        for k in range(KVH):
            cols = slice(k * HD, (k + 1) * HD)
            keys = [page[0, 0, :, cols] for page in pages]
            values = [page[0, 1, :, cols] for page in pages]
            if own:
                keys.append(fresh_ref[0, :, cols])
                values.append(fresh_ref[1, :, cols])
            scores.append(dot_t(held[t, k, :ROWS, :], jnp.concatenate(keys, axis=0)))
            vals.append(jnp.concatenate(values, axis=0))
        if own:
            fresh_alive = (
                (lax.div(token, STEPS) == owner)
                & (lax.rem(token, STEPS) <= lax.rem(step, STEPS))
                & (token < RS)
            )
        weights = []
        for s in scores:
            parts = [
                jnp.where(token < bounds[c], s[:, c * PAGE : (c + 1) * PAGE], LOWEST)
                for c in range(MAXP)
            ]
            if own:
                parts.append(jnp.where(fresh_alive, s[:, MAXP * PAGE :], LOWEST))
            top = jnp.max(functools.reduce(jnp.maximum, parts), axis=-1, keepdims=True)
            m = jnp.maximum(jnp.broadcast_to(top, (ROWS, HD)), FLOOR) * LOG2
            p = [jnp.exp2(part * LOG2 - m).astype(BF16) for part in parts]
            weights.append((m, jnp.concatenate(p, axis=1)))
        for k, ((m, p), v) in enumerate(zip(weights, vals)):
            pv = jnp.dot(
                p,
                jnp.concatenate([v, jnp.ones_like(v)], axis=1),
                preferred_element_type=F32,
            )
            found[k, :ROWS, :] = pv[:, :HD].astype(BF16)
            found[k, ROWS:, :] = pack_stats(m, pv[:, HD:])

    if first:
        attend(False)
    else:

        @pl.when(t == 0)
        def _():
            attend(True)

        @pl.when(t != 0)
        def _():
            attend(False)

    for n, out_ref in enumerate(out_refs):

        @pl.when(t == n)
        def _():
            out_ref[...] = found[...]


def page_part(at, slots, asked, first, fresh, pool):
    n = len(asked)

    def page_spec(c):
        return pl.BlockSpec(
            (1, 2, PAGE, KVH * HD),
            lambda t, at, slot: (slot[0, (at[2] ^ (first + t)) * MAXP + c], 0, 0, 0),
        )

    return pl.pallas_call(
        functools.partial(page_kernel, first=first),
        grid_spec=pltpu.PrefetchScalarGridSpec(
            num_scalar_prefetch=2,
            grid=(n,),
            in_specs=[pl.BlockSpec(asked[0].shape, lambda t, at, slot: (0, 0, 0))] * n
            + [pl.BlockSpec(fresh.shape, lambda t, at, slot: (0, 0, 0))]
            + [page_spec(c) for c in range(MAXP)],
            out_specs=[pl.BlockSpec((KVH, PACK, HD), lambda t, at, slot: (0, 0, 0))] * n,
            scratch_shapes=[
                pltpu.VMEM((n, *asked[0].shape), BF16),
                pltpu.VMEM((KVH, PACK, HD), BF16),
            ],
        ),
        out_shape=[jax.ShapeDtypeStruct((KVH, PACK, HD), BF16)] * n,
        compiler_params=pltpu.CompilerParams(vmem_limit_bytes=48 << 20),
        cost_estimate=pl.CostEstimate(
            flops=n * KVH * ROWS * MAXP * PAGE * HD * 16,
            bytes_accessed=4 << 20,
            transcendentals=n * KVH * ROWS * MAXP * PAGE,
        ),
        name="page_part",
    )(at, slots, *asked, fresh, *([pool] * MAXP))


def merge_kernel(part_ref, *rest):
    page_refs, out_ref = rest[:-1], rest[-1]
    found = [part_ref.at[0, i] for i in range(part_ref.shape[1])]
    found += [ref.at[0] for ref in page_refs]
    for half in range(ROWS // 128):
        stats = [unpack_stats(ref[ROWS:, :], half) for ref in found]
        top = functools.reduce(jnp.maximum, [m for m, _ in stats])
        fades = [jnp.exp2(m - top) for m, _ in stats]
        weight_sum = functools.reduce(jnp.add, [l * f for (_, l), f in zip(stats, fades)])
        gains = jnp.concatenate(
            [f / weight_sum for f in fades] + [jnp.zeros((128 - len(fades), 128), F32)], axis=0
        ).T
        total = jnp.zeros((128, HD), F32)
        for i, ref in enumerate(found):
            gain = jnp.broadcast_to(gains[:, i : i + 1], (128, HD))
            total = total + ref[half * 128 : half * 128 + 128, :].astype(F32) * gain
        total = total.astype(BF16)
        for j in range(128 // RS):
            col = half * 128 // RS + j
            rows = total[j * RS : (j + 1) * RS].reshape(REQ, STEPS, HD)
            out_ref[:, :, col * HD : (col + 1) * HD] = rows


def merge(parts, pages):
    return pl.pallas_call(
        merge_kernel,
        grid=(KVH,),
        in_specs=[pl.BlockSpec((1, *parts.shape[1:]), lambda k: (k, 0, 0, 0))]
        + [pl.BlockSpec((1, PACK, HD), lambda k: (k, 0, 0))] * len(pages),
        out_specs=pl.BlockSpec((REQ, STEPS, GQA * HD), lambda k: (0, 0, k)),
        out_shape=jax.ShapeDtypeStruct((REQ, STEPS, HQ * HD), BF16),
        compiler_params=pltpu.CompilerParams(vmem_limit_bytes=32 << 20),
        name="merge",
    )(parts, *pages)


def swap(x, axis, mask):
    return lax.ppermute(x, axis, [(i, i ^ mask) for i in range(lax.axis_size(axis))])


def fetch(x, axis, by):
    n = lax.axis_size(axis)
    return lax.ppermute(x, axis, [((i + by) % n, i) for i in range(n)])


def after(x, *done):
    return lax.optimization_barrier((x, *done))[0]


def local(queries, prefix_kv, pool, new_kv, unique_len, page_table, send_slots):
    at = jnp.stack([lax.axis_index(name) for name in ("y", "z", "grp")])
    asked, dealt = prep(page_table, unique_len, queries, prefix_kv)
    tokens = prefix_kv.shape[1]
    dealt = dealt.reshape(2 * KVH, 2, tokens, HD)
    kv_all = lax.all_to_all(dealt, ("xl", "z"), 0, 0, tiled=True)
    chunks = [asked] + [fetch(asked, "y", k) for k in (1, 2, 3)]
    asked_1 = swap(asked, "grp", 1)
    asked_2 = swap(asked, "grp", 2)
    asked_3 = swap(asked_1, "grp", 2)
    fresh = new_kv.transpose(2, 0, 1, 3).reshape(2, RS, KVH * HD)
    fresh = jnp.pad(fresh, ((0, 0), (0, PAGE - RS), (0, 0)))
    near = page_part(at, send_slots, [asked, asked_1], 0, fresh, pool)
    mine, *sent = pick(after(at, near[0]), chunks)
    came = [fetch(x, "z", k) for k, x in enumerate(sent, 1)]
    part = prefix_part(at, [mine], kv_all, 0, [], 256)
    part = prefix_part(at, came, kv_all, 1, [part], 256)
    part = after(part, asked_2, asked_3)
    moved = lax.all_to_all(part, ("z", "y"), 0, 0, tiled=True)
    far = page_part(after(at, part), send_slots, [asked_2, asked_3], 2, fresh, pool)
    far_came = [swap(x, "grp", 2 + n) for n, x in enumerate(far)]
    pages = [near[0], swap(near[1], "grp", 1), *far_came]
    return merge(moved.reshape(KVH, 4, PACK, HD), pages)


def solution(mesh):
    fine = Mesh(mesh.devices.reshape(4, 4, 2, 4), AXES)
    every = P(AXES)
    dev = ("y", "xl", "z")
    placed = (every, P("grp", dev), every, every, every, every, every)
    return jax.shard_map(local, mesh=fine, in_specs=placed, out_specs=every, check_vma=False)
```

```python
import functools
import math

import jax
import jax.numpy as jnp
from jax import lax
from jax.experimental import pallas as pl
from jax.experimental.pallas import tpu as pltpu
from jax.sharding import Mesh, PartitionSpec as P

HQ = 64
KVH = 4
HD = 128
GQA = 16
STEPS = 4
PAGE = 128
MAXP = 6
REQ = 4
RS = REQ * STEPS
ROWS = RS * GQA
PACK = ROWS + 16
FLOOR = -1e29
LOWEST = -1e30
LOG2 = math.log2(math.e) / math.sqrt(HD)
AXES = ("grp", "y", "xl", "z")
F32 = jnp.float32
BF16 = jnp.bfloat16


def dot_t(a, b):
    return lax.dot_general(a, b, (((1,), (1,)), ((), ())), preferred_element_type=F32)


def split3(x):
    hi = x.astype(BF16).astype(F32)
    rest = x - hi
    mid = rest.astype(BF16).astype(F32)
    return hi, mid, rest - mid


def pack_stats(m, l):
    lane = lax.broadcasted_iota(jnp.int32, (128, 128), 1)
    row = lax.broadcasted_iota(jnp.int32, (8, 128), 0)
    parts = []
    for half in range(ROWS // 128):
        rows = slice(half * 128, half * 128 + 128)
        both = jnp.where(lane < 64, m[rows], l[rows]).T
        stats = jnp.zeros((8, 128), F32)
        for i, found in enumerate(split3(both[:8]) + split3(both[64:72])):
            stats = jnp.where(row == i, found, stats)
        parts.append(stats)
    return jnp.concatenate(parts, axis=0).astype(BF16)


def unpack_stats(packed, half):
    wide = packed.astype(F32)[half * 8 : half * 8 + 8]
    return wide[0:1] + wide[1:2] + wide[2:3], wide[3:4] + wide[4:5] + wide[5:6]


def widen(x, width):
    return jnp.concatenate([x] * (width // HD), axis=1)


def scaled(q):
    wide = q.astype(F32) * LOG2
    high = wide.astype(BF16)
    return jnp.concatenate([high, (wide - high.astype(F32)).astype(BF16)], axis=1)


def online(q, kv_ref, tile):
    m = l = o = None
    q = scaled(q)
    blocks, _, tokens, _ = kv_ref.shape
    for b in range(blocks):
        for t in range(0, tokens, tile):
            k = kv_ref[b, 0, t : t + tile, :]
            v = kv_ref[b, 1, t : t + tile, :]
            s = dot_t(q, jnp.concatenate([k, k], axis=1))
            top = jnp.broadcast_to(jnp.max(s, axis=-1, keepdims=True), (q.shape[0], HD))
            new = top if m is None else jnp.maximum(m, top)
            p = jnp.exp2(s - widen(new, tile))
            pv = jnp.dot(
                p.astype(BF16),
                jnp.concatenate([v, jnp.ones_like(v)], axis=1),
                preferred_element_type=F32,
            )
            if m is None:
                l, o = pv[:, HD:], pv[:, :HD]
            else:
                fade = jnp.exp2(m - new)
                l, o = l * fade + pv[:, HD:], o * fade + pv[:, :HD]
            m = new
    return m, l, o


def prefix_kernel(at_ref, *refs, count, tile):
    q_refs, kv_ref, out_ref, held = refs[:count], refs[count], refs[-2], refs[-1]
    i = pl.program_id(0)

    @pl.when(i == 0)
    def _():
        for n, q_ref in enumerate(q_refs):
            held[n] = q_ref[...].reshape(4 * ROWS, HD)

    m, l, o = online(held[i], kv_ref, tile)
    for n in range(4):
        part = slice(n * ROWS, (n + 1) * ROWS)
        place = lax.rem(at_ref[0] + n, 4)
        out_ref[place, :ROWS, :] = o[part].astype(BF16)
        out_ref[place, ROWS:, :] = pack_stats(m[part], l[part])


def prefix_part(at, qs, kv, first, done, tile):
    count = len(qs)
    tokens = kv.shape[0] * kv.shape[2]
    return pl.pallas_call(
        functools.partial(prefix_kernel, count=count, tile=tile),
        grid_spec=pltpu.PrefetchScalarGridSpec(
            num_scalar_prefetch=1,
            grid=(count,),
            in_specs=[pl.BlockSpec(qs[0].shape, lambda i, at: (0, 0, 0))] * count
            + [pl.BlockSpec(kv.shape, lambda i, at: (0, 0, 0, 0))]
            + [pl.BlockSpec(memory_space=pl.ANY)] * len(done),
            out_specs=pl.BlockSpec(
                (4, PACK, HD), lambda i, at: (lax.rem(at[1] + i + first, 4), 0, 0)
            ),
            scratch_shapes=[pltpu.VMEM((count, 4 * ROWS, HD), BF16)],
        ),
        out_shape=jax.ShapeDtypeStruct((16, PACK, HD), BF16),
        input_output_aliases={count + 2: 0} if done else {},
        compiler_params=pltpu.CompilerParams(vmem_limit_bytes=48 << 20),
        cost_estimate=pl.CostEstimate(
            flops=count * ROWS * tokens * HD * 32,
            bytes_accessed=8 << 20,
            transcendentals=count * ROWS * tokens * 4,
        ),
        name="prefix_part",
    )(at, *qs, kv, *done)


def prep_kernel(table_ref, size_ref, q_ref, kv_ref, asked_ref, dealt_ref):
    for c in range(GQA):
        tile = q_ref[:, :, c * HD : (c + 1) * HD].reshape(RS, HD)
        asked_ref[0, c * RS : (c + 1) * RS, :] = tile
    both = kv_ref[0].astype(F32)
    for i in range(2):
        half = both[:, i].astype(BF16)
        dealt_ref[0, 0, i] = half
        dealt_ref[1, 0, i] = half

    @pl.when(pl.program_id(0) == 0)
    def _():
        lane = lax.broadcasted_iota(jnp.int32, (16, HD), 1)
        row = lax.broadcasted_iota(jnp.int32, (16, HD), 0)
        notes = jnp.zeros((16, HD), jnp.int32)
        for slot in range(REQ * MAXP):
            req, page = divmod(slot, MAXP)
            alive = jnp.clip(size_ref[0:1, req : req + 1] - page * PAGE, 0, PAGE)
            here = jnp.where(row == 0, req, jnp.where(row == 1, alive, 0))
            notes = jnp.where(lane == table_ref[0:1, slot : slot + 1], here, notes)
        asked_ref[0, ROWS:, :] = notes.astype(F32).astype(BF16)

    @pl.when(pl.program_id(0) != 0)
    def _():
        asked_ref[0, ROWS:, :] = jnp.zeros((16, HD), BF16)


def prep(page_table, unique_len, queries, prefix_kv):
    tokens = prefix_kv.shape[1]
    return pl.pallas_call(
        prep_kernel,
        grid=(KVH,),
        in_specs=[
            pl.BlockSpec(page_table.shape, lambda k: (0, 0)),
            pl.BlockSpec((1, REQ), lambda k: (0, 0)),
            pl.BlockSpec((REQ, STEPS, GQA * HD), lambda k: (0, 0, k)),
            pl.BlockSpec((1, tokens, 2, HD), lambda k: (0, 0, 0, k)),
        ],
        out_specs=[
            pl.BlockSpec((1, PACK, HD), lambda k: (k, 0, 0)),
            pl.BlockSpec((2, 1, 2, tokens, HD), lambda k: (0, k, 0, 0, 0)),
        ],
        out_shape=[
            jax.ShapeDtypeStruct((KVH, PACK, HD), BF16),
            jax.ShapeDtypeStruct((2, KVH, 2, tokens, HD), BF16),
        ],
        compiler_params=pltpu.CompilerParams(vmem_limit_bytes=60 << 20),
        name="prep",
    )(page_table, unique_len.reshape(1, REQ), queries, prefix_kv)


def pick_kernel(at_ref, *refs):
    q_refs, out_refs = refs[:4], refs[4:]
    for k, out_ref in enumerate(out_refs):
        head = lax.rem(at_ref[1] + 4 - k, 4)
        for n, q_ref in enumerate(q_refs):
            out_ref[n] = q_ref[head, :ROWS, :]


def pick(at, asked):
    scalar = pl.BlockSpec(memory_space=pltpu.SMEM)
    whole = pl.BlockSpec(memory_space=pltpu.VMEM)
    return pl.pallas_call(
        pick_kernel,
        in_specs=[scalar] + [whole] * 4,
        out_specs=[whole] * 4,
        out_shape=[jax.ShapeDtypeStruct((4, ROWS, HD), BF16)] * 4,
        compiler_params=pltpu.CompilerParams(vmem_limit_bytes=32 << 20),
        name="pick",
    )(at, *asked)


def page_kernel(at_ref, slot_ref, *refs, first):
    count = (len(refs) - MAXP - 3) // 2
    q_refs, fresh_ref, pages = refs[:count], refs[count], refs[count + 1 : count + 1 + MAXP]
    out_refs, (held, found) = refs[count + 1 + MAXP : -2], refs[-2:]
    t = pl.program_id(0)

    @pl.when(t == 0)
    def _():
        for n, q_ref in enumerate(q_refs):
            held[n] = q_ref[...]

    row = lax.broadcasted_iota(jnp.int32, (ROWS, PAGE), 0)
    token = lax.broadcasted_iota(jnp.int32, (ROWS, PAGE), 1)
    step = lax.rem(row, RS)
    owner = lax.div(step, STEPS)
    notes = held[t, 0, ROWS:, :].astype(F32)
    place = lax.broadcasted_iota(jnp.int32, (1, HD), 1)
    bounds = []
    for c in range(MAXP):
        here = place == at_ref[2] * MAXP + c
        req, size = (
            jnp.sum(jnp.where(here, notes[i : i + 1], 0.0), axis=1, keepdims=True).astype(jnp.int32)
            for i in range(2)
        )
        bounds.append(jnp.where(owner == req, size, 0))

    def attend(own):
        scores, vals = [], []
        for k in range(KVH):
            cols = slice(k * HD, (k + 1) * HD)
            keys = [page[0, 0, :, cols] for page in pages]
            values = [page[0, 1, :, cols] for page in pages]
            if own:
                keys.append(fresh_ref[0, :, cols])
                values.append(fresh_ref[1, :, cols])
            scores.append(dot_t(held[t, k, :ROWS, :], jnp.concatenate(keys, axis=0)))
            vals.append(jnp.concatenate(values, axis=0))
        if own:
            fresh_alive = (
                (lax.div(token, STEPS) == owner)
                & (lax.rem(token, STEPS) <= lax.rem(step, STEPS))
                & (token < RS)
            )
        weights = []
        for s in scores:
            parts = [
                jnp.where(token < bounds[c], s[:, c * PAGE : (c + 1) * PAGE], LOWEST)
                for c in range(MAXP)
            ]
            if own:
                parts.append(jnp.where(fresh_alive, s[:, MAXP * PAGE :], LOWEST))
            top = jnp.max(functools.reduce(jnp.maximum, parts), axis=-1, keepdims=True)
            m = jnp.maximum(jnp.broadcast_to(top, (ROWS, HD)), FLOOR) * LOG2
            p = [jnp.exp2(part * LOG2 - m).astype(BF16) for part in parts]
            weights.append((m, jnp.concatenate(p, axis=1)))
        for k, ((m, p), v) in enumerate(zip(weights, vals)):
            pv = jnp.dot(
                p,
                jnp.concatenate([v, jnp.ones_like(v)], axis=1),
                preferred_element_type=F32,
            )
            found[k, :ROWS, :] = pv[:, :HD].astype(BF16)
            found[k, ROWS:, :] = pack_stats(m, pv[:, HD:])

    if first:
        attend(False)
    else:

        @pl.when(t == 0)
        def _():
            attend(True)

        @pl.when(t != 0)
        def _():
            attend(False)

    for n, out_ref in enumerate(out_refs):

        @pl.when(t == n)
        def _():
            out_ref[...] = found[...]


def page_part(at, slots, asked, first, fresh, pool):
    n = len(asked)

    def page_spec(c):
        return pl.BlockSpec(
            (1, 2, PAGE, KVH * HD),
            lambda t, at, slot: (slot[0, (at[2] ^ (first + t)) * MAXP + c], 0, 0, 0),
        )

    return pl.pallas_call(
        functools.partial(page_kernel, first=first),
        grid_spec=pltpu.PrefetchScalarGridSpec(
            num_scalar_prefetch=2,
            grid=(n,),
            in_specs=[pl.BlockSpec(asked[0].shape, lambda t, at, slot: (0, 0, 0))] * n
            + [pl.BlockSpec(fresh.shape, lambda t, at, slot: (0, 0, 0))]
            + [page_spec(c) for c in range(MAXP)],
            out_specs=[pl.BlockSpec((KVH, PACK, HD), lambda t, at, slot: (0, 0, 0))] * n,
            scratch_shapes=[
                pltpu.VMEM((n, *asked[0].shape), BF16),
                pltpu.VMEM((KVH, PACK, HD), BF16),
            ],
        ),
        out_shape=[jax.ShapeDtypeStruct((KVH, PACK, HD), BF16)] * n,
        compiler_params=pltpu.CompilerParams(vmem_limit_bytes=48 << 20),
        cost_estimate=pl.CostEstimate(
            flops=n * KVH * ROWS * MAXP * PAGE * HD * 64,
            bytes_accessed=4 << 20,
            transcendentals=n * KVH * ROWS * MAXP * PAGE,
        ),
        name="page_part",
    )(at, slots, *asked, fresh, *([pool] * MAXP))


def merge_kernel(part_ref, *rest):
    page_refs, out_ref = rest[:-1], rest[-1]
    found = [part_ref.at[0, i] for i in range(part_ref.shape[1])]
    found += [ref.at[0] for ref in page_refs]
    for half in range(ROWS // 128):
        stats = [unpack_stats(ref[ROWS:, :], half) for ref in found]
        top = functools.reduce(jnp.maximum, [m for m, _ in stats])
        fades = [jnp.exp2(m - top) for m, _ in stats]
        weight_sum = functools.reduce(jnp.add, [l * f for (_, l), f in zip(stats, fades)])
        gains = jnp.concatenate(
            [f / weight_sum for f in fades] + [jnp.zeros((128 - len(fades), 128), F32)], axis=0
        ).T
        total = jnp.zeros((128, HD), F32)
        for i, ref in enumerate(found):
            gain = jnp.broadcast_to(gains[:, i : i + 1], (128, HD))
            total = total + ref[half * 128 : half * 128 + 128, :].astype(F32) * gain
        total = total.astype(BF16)
        for j in range(128 // RS):
            col = half * 128 // RS + j
            rows = total[j * RS : (j + 1) * RS].reshape(REQ, STEPS, HD)
            out_ref[:, :, col * HD : (col + 1) * HD] = rows


def merge(parts, pages):
    return pl.pallas_call(
        merge_kernel,
        grid=(KVH,),
        in_specs=[pl.BlockSpec((1, *parts.shape[1:]), lambda k: (k, 0, 0, 0))]
        + [pl.BlockSpec((1, PACK, HD), lambda k: (k, 0, 0))] * len(pages),
        out_specs=pl.BlockSpec((REQ, STEPS, GQA * HD), lambda k: (0, 0, k)),
        out_shape=jax.ShapeDtypeStruct((REQ, STEPS, HQ * HD), BF16),
        compiler_params=pltpu.CompilerParams(vmem_limit_bytes=32 << 20),
        name="merge",
    )(parts, *pages)


def swap(x, axis, mask):
    return lax.ppermute(x, axis, [(i, i ^ mask) for i in range(lax.axis_size(axis))])


def fetch(x, axis, by):
    n = lax.axis_size(axis)
    return lax.ppermute(x, axis, [((i + by) % n, i) for i in range(n)])


def after(x, *done):
    return lax.optimization_barrier((x, *done))[0]


def local(queries, prefix_kv, pool, new_kv, unique_len, page_table, send_slots):
    at = jnp.stack([lax.axis_index(name) for name in ("y", "z", "grp")])
    asked, dealt = prep(page_table, unique_len, queries, prefix_kv)
    tokens = prefix_kv.shape[1]
    dealt = dealt.reshape(2 * KVH, 2, tokens, HD)
    kv_all = lax.all_to_all(dealt, ("xl", "z"), 0, 0, tiled=True)
    chunks = [asked] + [fetch(asked, "y", k) for k in (1, 2, 3)]
    asked_1 = swap(asked, "grp", 1)
    fresh = new_kv.transpose(2, 0, 1, 3).reshape(2, RS, KVH * HD)
    fresh = jnp.pad(fresh, ((0, 0), (0, PAGE - RS), (0, 0)))
    near = page_part(at, send_slots, [asked, asked_1], 0, fresh, pool)
    mine, *sent = pick(after(at, near[0]), chunks)
    came = [fetch(x, "z", k) for k, x in enumerate(sent, 1)]
    asked_2 = swap(after(asked, mine), "grp", 2)
    asked_3 = swap(after(asked_1, mine), "grp", 2)
    part = prefix_part(at, [mine], kv_all, 0, [], 256)
    part = prefix_part(at, came, kv_all, 1, [part], 256)
    part = after(part, asked_2, asked_3)
    moved = lax.all_to_all(part, ("z", "y"), 0, 0, tiled=True)
    late = after(at, part)
    (page_2,) = page_part(late, send_slots, [asked_2], 2, fresh, pool)
    (page_3,) = page_part(late, send_slots, [asked_3], 3, fresh, pool)
    found = [near[0], swap(near[1], "grp", 1), swap(page_3, "grp", 3), swap(page_2, "grp", 2)]
    return merge(moved.reshape(KVH, 4, PACK, HD), found)


def solution(mesh):
    fine = Mesh(mesh.devices.reshape(4, 4, 2, 4), AXES)
    every = P(AXES)
    dev = ("y", "xl", "z")
    placed = (every, P("grp", dev), every, every, every, every, every)
    return jax.shard_map(local, mesh=fine, in_specs=placed, out_specs=every, check_vma=False)
```

```python
import functools
import math

import jax
import jax.numpy as jnp
from jax import lax
from jax.experimental import pallas as pl
from jax.experimental.pallas import tpu as pltpu
from jax.sharding import Mesh, PartitionSpec as P

HQ = 64
KVH = 4
HD = 128
GQA = 16
STEPS = 4
PAGE = 128
MAXP = 6
REQ = 4
RS = REQ * STEPS
ROWS = RS * GQA
PACK = ROWS + 16
FLOOR = -1e29
LOWEST = -1e30
LOG2 = math.log2(math.e) / math.sqrt(HD)
AXES = ("grp", "y", "xl", "z")
F32 = jnp.float32
BF16 = jnp.bfloat16


def dot_t(a, b):
    return lax.dot_general(a, b, (((1,), (1,)), ((), ())), preferred_element_type=F32)


def split3(x):
    hi = x.astype(BF16).astype(F32)
    rest = x - hi
    mid = rest.astype(BF16).astype(F32)
    return hi, mid, rest - mid


def pack_stats(m, l):
    lane = lax.broadcasted_iota(jnp.int32, (128, 128), 1)
    row = lax.broadcasted_iota(jnp.int32, (8, 128), 0)
    parts = []
    for half in range(ROWS // 128):
        rows = slice(half * 128, half * 128 + 128)
        both = jnp.where(lane < 64, m[rows], l[rows]).T
        stats = jnp.zeros((8, 128), F32)
        for i, found in enumerate(split3(both[:8]) + split3(both[64:72])):
            stats = jnp.where(row == i, found, stats)
        parts.append(stats)
    return jnp.concatenate(parts, axis=0).astype(BF16)


def unpack_stats(packed, half):
    wide = packed.astype(F32)[half * 8 : half * 8 + 8]
    return wide[0:1] + wide[1:2] + wide[2:3], wide[3:4] + wide[4:5] + wide[5:6]


def widen(x, width):
    return jnp.concatenate([x] * (width // HD), axis=1)


def scaled(q):
    wide = q.astype(F32) * LOG2
    high = wide.astype(BF16)
    return jnp.concatenate([high, (wide - high.astype(F32)).astype(BF16)], axis=1)


def online(q, kv_ref, tile):
    m = l = o = None
    q = scaled(q)
    blocks, _, tokens, _ = kv_ref.shape
    for b in range(blocks):
        for t in range(0, tokens, tile):
            k = kv_ref[b, 0, t : t + tile, :]
            v = kv_ref[b, 1, t : t + tile, :]
            s = dot_t(q, jnp.concatenate([k, k], axis=1))
            top = jnp.broadcast_to(jnp.max(s, axis=-1, keepdims=True), (q.shape[0], HD))
            new = top if m is None else jnp.maximum(m, top)
            p = jnp.exp2(s - widen(new, tile))
            pv = jnp.dot(
                p.astype(BF16),
                jnp.concatenate([v, jnp.ones_like(v)], axis=1),
                preferred_element_type=F32,
            )
            if m is None:
                l, o = pv[:, HD:], pv[:, :HD]
            else:
                fade = jnp.exp2(m - new)
                l, o = l * fade + pv[:, HD:], o * fade + pv[:, :HD]
            m = new
    return m, l, o


def prefix_kernel(at_ref, *refs, count, per, tile):
    q_refs, kv_ref, done_refs, (out_ref, held) = (
        refs[:count],
        refs[count],
        refs[count + 1 : -2],
        refs[-2:],
    )
    i = pl.program_id(0)
    first = len(done_refs)

    @pl.when(i == 0)
    def _():
        for n, q_ref in enumerate(q_refs):
            held[4 * n : 4 * n + 4] = q_ref[...]
        for done_ref in done_refs:
            for n in range(4):
                out_ref[4 * at_ref[1] + n] = done_ref[n]

    rows = held[pl.ds(i * per, per)].reshape(per * ROWS, HD)
    m, l, o = online(rows, kv_ref, tile)
    for n in range(per):
        part = slice(n * ROWS, (n + 1) * ROWS)
        block = i * per + n
        place = lax.rem(at_ref[0] + block, 4)
        if first:
            place = place + 4 * lax.rem(at_ref[1] + 1 + lax.div(block, 4), 4)
        out_ref[place, :ROWS, :] = o[part].astype(BF16)
        out_ref[place, ROWS:, :] = pack_stats(m[part], l[part])


def prefix_part(at, qs, kv, done, per, tile):
    count = len(qs)
    blocks = 16 if done else 4
    tokens = kv.shape[0] * kv.shape[2]
    return pl.pallas_call(
        functools.partial(prefix_kernel, count=count, per=per, tile=tile),
        grid_spec=pltpu.PrefetchScalarGridSpec(
            num_scalar_prefetch=1,
            grid=(4 * count // per,),
            in_specs=[pl.BlockSpec(qs[0].shape, lambda i, at: (0, 0, 0))] * count
            + [pl.BlockSpec(kv.shape, lambda i, at: (0, 0, 0, 0))]
            + [pl.BlockSpec((4, PACK, HD), lambda i, at: (0, 0, 0))] * len(done),
            out_specs=pl.BlockSpec((blocks, PACK, HD), lambda i, at: (0, 0, 0)),
            scratch_shapes=[pltpu.VMEM((4 * count, ROWS, HD), BF16)],
        ),
        out_shape=jax.ShapeDtypeStruct((blocks, PACK, HD), BF16),
        compiler_params=pltpu.CompilerParams(vmem_limit_bytes=48 << 20),
        cost_estimate=pl.CostEstimate(
            flops=count * ROWS * tokens * HD * 32,
            bytes_accessed=8 << 20,
            transcendentals=count * ROWS * tokens * 4,
        ),
        name="prefix_part",
    )(at, *qs, kv, *done)


def prep_kernel(table_ref, size_ref, q_ref, kv_ref, asked_ref, rows_ref, dealt_ref):
    for c in range(GQA):
        tile = q_ref[:, :, c * HD : (c + 1) * HD].reshape(RS, HD)
        asked_ref[0, c * RS : (c + 1) * RS, :] = tile
        rows_ref[0, c * RS : (c + 1) * RS, :] = tile
    both = kv_ref[0].astype(F32)
    for i in range(2):
        half = both[:, i].astype(BF16)
        dealt_ref[0, 0, i] = half
        dealt_ref[1, 0, i] = half

    @pl.when(pl.program_id(0) == 0)
    def _():
        lane = lax.broadcasted_iota(jnp.int32, (16, HD), 1)
        row = lax.broadcasted_iota(jnp.int32, (16, HD), 0)
        notes = jnp.zeros((16, HD), jnp.int32)
        for slot in range(REQ * MAXP):
            req, page = divmod(slot, MAXP)
            alive = jnp.clip(size_ref[0:1, req : req + 1] - page * PAGE, 0, PAGE)
            here = jnp.where(row == 0, req, jnp.where(row == 1, alive, 0))
            notes = jnp.where(lane == table_ref[0:1, slot : slot + 1], here, notes)
        asked_ref[0, ROWS:, :] = notes.astype(F32).astype(BF16)

    @pl.when(pl.program_id(0) != 0)
    def _():
        asked_ref[0, ROWS:, :] = jnp.zeros((16, HD), BF16)


def prep(page_table, unique_len, queries, prefix_kv):
    tokens = prefix_kv.shape[1]
    return pl.pallas_call(
        prep_kernel,
        grid=(KVH,),
        in_specs=[
            pl.BlockSpec(page_table.shape, lambda k: (0, 0)),
            pl.BlockSpec((1, REQ), lambda k: (0, 0)),
            pl.BlockSpec((REQ, STEPS, GQA * HD), lambda k: (0, 0, k)),
            pl.BlockSpec((1, tokens, 2, HD), lambda k: (0, 0, 0, k)),
        ],
        out_specs=[
            pl.BlockSpec((1, PACK, HD), lambda k: (k, 0, 0)),
            pl.BlockSpec((1, ROWS, HD), lambda k: (k, 0, 0)),
            pl.BlockSpec((2, 1, 2, tokens, HD), lambda k: (0, k, 0, 0, 0)),
        ],
        out_shape=[
            jax.ShapeDtypeStruct((KVH, PACK, HD), BF16),
            jax.ShapeDtypeStruct((KVH, ROWS, HD), BF16),
            jax.ShapeDtypeStruct((2, KVH, 2, tokens, HD), BF16),
        ],
        compiler_params=pltpu.CompilerParams(vmem_limit_bytes=60 << 20),
        name="prep",
    )(page_table, unique_len.reshape(1, REQ), queries, prefix_kv)


def pick_kernel(at_ref, *refs):
    q_refs, out_refs = refs[:4], refs[4:]
    for k, out_ref in enumerate(out_refs):
        head = lax.rem(at_ref[1] + 4 - k, 4)
        for n, q_ref in enumerate(q_refs):
            out_ref[n] = q_ref[head]


def pick(at, asked):
    scalar = pl.BlockSpec(memory_space=pltpu.SMEM)
    whole = pl.BlockSpec(memory_space=pltpu.VMEM)
    return pl.pallas_call(
        pick_kernel,
        in_specs=[scalar] + [whole] * 4,
        out_specs=[whole] * 4,
        out_shape=[jax.ShapeDtypeStruct((4, ROWS, HD), BF16)] * 4,
        compiler_params=pltpu.CompilerParams(vmem_limit_bytes=32 << 20),
        name="pick",
    )(at, *asked)


def page_kernel(at_ref, slot_ref, *refs, first):
    count = (len(refs) - MAXP - 3) // 2
    q_refs, fresh_ref, pages = refs[:count], refs[count], refs[count + 1 : count + 1 + MAXP]
    out_refs, (held, found) = refs[count + 1 + MAXP : -2], refs[-2:]
    t = pl.program_id(0)

    @pl.when(t == 0)
    def _():
        for n, q_ref in enumerate(q_refs):
            held[n] = q_ref[...]

    row = lax.broadcasted_iota(jnp.int32, (ROWS, PAGE), 0)
    token = lax.broadcasted_iota(jnp.int32, (ROWS, PAGE), 1)
    step = lax.rem(row, RS)
    owner = lax.div(step, STEPS)
    notes = held[t, 0, ROWS:, :].astype(F32)
    place = lax.broadcasted_iota(jnp.int32, (1, HD), 1)
    bounds = []
    for c in range(MAXP):
        here = place == at_ref[2] * MAXP + c
        req, size = (
            jnp.sum(jnp.where(here, notes[i : i + 1], 0.0), axis=1, keepdims=True).astype(jnp.int32)
            for i in range(2)
        )
        bounds.append(jnp.where(owner == req, size, 0))

    def attend(own):
        scores, vals = [], []
        for k in range(KVH):
            cols = slice(k * HD, (k + 1) * HD)
            keys = [page[0, 0, :, cols] for page in pages]
            values = [page[0, 1, :, cols] for page in pages]
            if own:
                keys.append(fresh_ref[0, :, cols])
                values.append(fresh_ref[1, :, cols])
            scores.append(dot_t(held[t, k, :ROWS, :], jnp.concatenate(keys, axis=0)))
            vals.append(jnp.concatenate(values, axis=0))
        if own:
            fresh_alive = (
                (lax.div(token, STEPS) == owner)
                & (lax.rem(token, STEPS) <= lax.rem(step, STEPS))
                & (token < RS)
            )
        weights = []
        for s in scores:
            parts = [
                jnp.where(token < bounds[c], s[:, c * PAGE : (c + 1) * PAGE], LOWEST)
                for c in range(MAXP)
            ]
            if own:
                parts.append(jnp.where(fresh_alive, s[:, MAXP * PAGE :], LOWEST))
            top = jnp.max(functools.reduce(jnp.maximum, parts), axis=-1, keepdims=True)
            m = jnp.maximum(jnp.broadcast_to(top, (ROWS, HD)), FLOOR) * LOG2
            p = [jnp.exp2(part * LOG2 - m).astype(BF16) for part in parts]
            weights.append((m, jnp.concatenate(p, axis=1)))
        for k, ((m, p), v) in enumerate(zip(weights, vals)):
            pv = jnp.dot(
                p,
                jnp.concatenate([v, jnp.ones_like(v)], axis=1),
                preferred_element_type=F32,
            )
            found[k, :ROWS, :] = pv[:, :HD].astype(BF16)
            found[k, ROWS:, :] = pack_stats(m, pv[:, HD:])

    if first:
        attend(False)
    else:

        @pl.when(t == 0)
        def _():
            attend(True)

        @pl.when(t != 0)
        def _():
            attend(False)

    for n, out_ref in enumerate(out_refs):

        @pl.when(t == n)
        def _():
            out_ref[...] = found[...]


def page_part(at, slots, asked, first, fresh, pool):
    n = len(asked)

    def page_spec(c):
        return pl.BlockSpec(
            (1, 2, PAGE, KVH * HD),
            lambda t, at, slot: (slot[0, (at[2] ^ (first + t)) * MAXP + c], 0, 0, 0),
        )

    return pl.pallas_call(
        functools.partial(page_kernel, first=first),
        grid_spec=pltpu.PrefetchScalarGridSpec(
            num_scalar_prefetch=2,
            grid=(n,),
            in_specs=[pl.BlockSpec(asked[0].shape, lambda t, at, slot: (0, 0, 0))] * n
            + [pl.BlockSpec(fresh.shape, lambda t, at, slot: (0, 0, 0))]
            + [page_spec(c) for c in range(MAXP)],
            out_specs=[pl.BlockSpec((KVH, PACK, HD), lambda t, at, slot: (0, 0, 0))] * n,
            scratch_shapes=[
                pltpu.VMEM((n, *asked[0].shape), BF16),
                pltpu.VMEM((KVH, PACK, HD), BF16),
            ],
        ),
        out_shape=[jax.ShapeDtypeStruct((KVH, PACK, HD), BF16)] * n,
        compiler_params=pltpu.CompilerParams(vmem_limit_bytes=48 << 20),
        cost_estimate=pl.CostEstimate(
            flops=n * KVH * ROWS * MAXP * PAGE * HD * 64,
            bytes_accessed=4 << 20,
            transcendentals=n * KVH * ROWS * MAXP * PAGE,
        ),
        name="page_part",
    )(at, slots, *asked, fresh, *([pool] * MAXP))


def merge_kernel(part_ref, *rest):
    page_refs, out_ref = rest[:-1], rest[-1]
    for head in range(part_ref.shape[0]):
        found = [part_ref.at[head, i] for i in range(part_ref.shape[1])]
        found += [ref.at[head] for ref in page_refs]
        for half in range(ROWS // 128):
            stats = [unpack_stats(ref[ROWS:, :], half) for ref in found]
            top = functools.reduce(jnp.maximum, [m for m, _ in stats])
            fades = [jnp.exp2(m - top) for m, _ in stats]
            weight_sum = functools.reduce(jnp.add, [l * f for (_, l), f in zip(stats, fades)])
            gains = jnp.concatenate(
                [f / weight_sum for f in fades] + [jnp.zeros((128 - len(fades), 128), F32)], axis=0
            ).T
            total = jnp.zeros((128, HD), F32)
            for i, ref in enumerate(found):
                gain = jnp.broadcast_to(gains[:, i : i + 1], (128, HD))
                total = total + ref[half * 128 : half * 128 + 128, :].astype(F32) * gain
            total = total.astype(BF16)
            for j in range(128 // RS):
                col = head * GQA + half * 128 // RS + j
                rows = total[j * RS : (j + 1) * RS].reshape(REQ, STEPS, HD)
                out_ref[:, :, col * HD : (col + 1) * HD] = rows


def merge(parts, pages):
    heads = 2
    return pl.pallas_call(
        merge_kernel,
        grid=(KVH // heads,),
        in_specs=[pl.BlockSpec((heads, *parts.shape[1:]), lambda k: (k, 0, 0, 0))]
        + [pl.BlockSpec((heads, PACK, HD), lambda k: (k, 0, 0))] * len(pages),
        out_specs=pl.BlockSpec((REQ, STEPS, heads * GQA * HD), lambda k: (0, 0, k)),
        out_shape=jax.ShapeDtypeStruct((REQ, STEPS, HQ * HD), BF16),
        compiler_params=pltpu.CompilerParams(vmem_limit_bytes=32 << 20),
        name="merge",
    )(parts, *pages)


def swap(x, axis, mask):
    return lax.ppermute(x, axis, [(i, i ^ mask) for i in range(lax.axis_size(axis))])


def fetch(x, axis, by):
    n = lax.axis_size(axis)
    return lax.ppermute(x, axis, [((i + by) % n, i) for i in range(n)])


def after(x, *done):
    return lax.optimization_barrier((x, *done))[0]


def local(queries, prefix_kv, pool, new_kv, unique_len, page_table, send_slots):
    at = jnp.stack([lax.axis_index(name) for name in ("y", "z", "grp")])
    asked, rows, dealt = prep(page_table, unique_len, queries, prefix_kv)
    tokens = prefix_kv.shape[1]
    dealt = dealt.reshape(2 * KVH, 2, tokens, HD)
    kv_all = lax.all_to_all(dealt, ("xl", "z"), 0, 0, tiled=True)
    chunks = [rows] + [fetch(rows, "y", k) for k in (1, 2, 3)]
    asked_1 = swap(asked, "grp", 1)
    fresh = new_kv.transpose(2, 0, 1, 3).reshape(2, RS, KVH * HD)
    fresh = jnp.pad(fresh, ((0, 0), (0, PAGE - RS), (0, 0)))
    near = page_part(at, send_slots, [asked, asked_1], 0, fresh, pool)
    mine, *sent = pick(after(at, near[0]), chunks)
    came = [fetch(x, "z", k) for k, x in enumerate(sent, 1)]
    asked_2 = swap(after(asked, mine), "grp", 2)
    asked_3 = swap(after(asked_1, mine), "grp", 2)
    part = prefix_part(at, [mine], kv_all, [], 4, 256)
    part = prefix_part(at, came, kv_all, [part], 6, 256)
    part = after(part, asked_2, asked_3)
    moved = lax.all_to_all(part, ("z", "y"), 0, 0, tiled=True)
    late = after(at, part)
    (page_2,) = page_part(late, send_slots, [asked_2], 2, fresh, pool)
    (page_3,) = page_part(late, send_slots, [asked_3], 3, fresh, pool)
    found = [near[0], swap(near[1], "grp", 1), swap(page_3, "grp", 3), swap(page_2, "grp", 2)]
    return merge(moved.reshape(KVH, 4, PACK, HD), found)


def solution(mesh):
    fine = Mesh(mesh.devices.reshape(4, 4, 2, 4), AXES)
    every = P(AXES)
    dev = ("y", "xl", "z")
    placed = (every, P("grp", dev), every, every, every, every, every)
    return jax.shard_map(local, mesh=fine, in_specs=placed, out_specs=every, check_vma=False)
```

```python
import functools
import math

import jax
import jax.numpy as jnp
from jax import lax
from jax.experimental import pallas as pl
from jax.experimental.pallas import tpu as pltpu
from jax.sharding import Mesh, PartitionSpec as P

HQ = 64
KVH = 4
HD = 128
GQA = 16
STEPS = 4
PAGE = 128
MAXP = 6
REQ = 4
RS = REQ * STEPS
ROWS = RS * GQA
PACK = ROWS + 16
FLOOR = -1e29
LOWEST = -1e30
LOG2 = math.log2(math.e) / math.sqrt(HD)
AXES = ("grp", "y", "xl", "z")
F32 = jnp.float32
BF16 = jnp.bfloat16


def dot_t(a, b):
    return lax.dot_general(a, b, (((1,), (1,)), ((), ())), preferred_element_type=F32)


def split3(x):
    hi = x.astype(BF16).astype(F32)
    rest = x - hi
    mid = rest.astype(BF16).astype(F32)
    return hi, mid, rest - mid


def pack_stats(m, l):
    lane = lax.broadcasted_iota(jnp.int32, (128, 128), 1)
    row = lax.broadcasted_iota(jnp.int32, (8, 128), 0)
    parts = []
    for half in range(ROWS // 128):
        rows = slice(half * 128, half * 128 + 128)
        both = jnp.where(lane < 64, m[rows], l[rows]).T
        stats = jnp.zeros((8, 128), F32)
        for i, found in enumerate(split3(both[:8]) + split3(both[64:72])):
            stats = jnp.where(row == i, found, stats)
        parts.append(stats)
    return jnp.concatenate(parts, axis=0).astype(BF16)


def unpack_stats(packed, half):
    wide = packed.astype(F32)[half * 8 : half * 8 + 8]
    return wide[0:1] + wide[1:2] + wide[2:3], wide[3:4] + wide[4:5] + wide[5:6]


def widen(x, width):
    return jnp.concatenate([x] * (width // HD), axis=1)


def scaled(q):
    wide = q.astype(F32) * LOG2
    high = wide.astype(BF16)
    return jnp.concatenate([high, (wide - high.astype(F32)).astype(BF16)], axis=1)


def online(q, kv_ref, tile):
    m = l = o = None
    q = scaled(q)
    blocks, _, tokens, _ = kv_ref.shape
    for b in range(blocks):
        for t in range(0, tokens, tile):
            k = kv_ref[b, 0, t : t + tile, :]
            v = kv_ref[b, 1, t : t + tile, :]
            s = dot_t(q, jnp.concatenate([k, k], axis=1))
            top = jnp.broadcast_to(jnp.max(s, axis=-1, keepdims=True), (q.shape[0], HD))
            new = top if m is None else jnp.maximum(m, top)
            p = jnp.exp2(s - widen(new, tile))
            pv = jnp.dot(
                p.astype(BF16),
                jnp.concatenate([v, jnp.ones_like(v)], axis=1),
                preferred_element_type=F32,
            )
            if m is None:
                l, o = pv[:, HD:], pv[:, :HD]
            else:
                fade = jnp.exp2(m - new)
                l, o = l * fade + pv[:, HD:], o * fade + pv[:, :HD]
            m = new
    return m, l, o


def prefix_kernel(at_ref, *refs, count, per, tile):
    q_refs, kv_ref, done_refs, (out_ref, held) = (
        refs[:count],
        refs[count],
        refs[count + 1 : -2],
        refs[-2:],
    )
    i = pl.program_id(0)
    first = len(done_refs)

    @pl.when(i == 0)
    def _():
        for n, q_ref in enumerate(q_refs):
            held[4 * n : 4 * n + 4] = q_ref[...]
        for done_ref in done_refs:
            for n in range(4):
                out_ref[4 * at_ref[1] + n] = done_ref[n]

    rows = held[pl.ds(i * per, per)].reshape(per * ROWS, HD)
    m, l, o = online(rows, kv_ref, tile)
    for n in range(per):
        part = slice(n * ROWS, (n + 1) * ROWS)
        block = i * per + n
        place = lax.rem(at_ref[0] + block, 4)
        if first:
            place = place + 4 * lax.rem(at_ref[1] + 1 + lax.div(block, 4), 4)
        out_ref[place, :ROWS, :] = o[part].astype(BF16)
        out_ref[place, ROWS:, :] = pack_stats(m[part], l[part])


def prefix_part(at, qs, kv, done, per, tile):
    count = len(qs)
    blocks = 16 if done else 4
    tokens = kv.shape[0] * kv.shape[2]
    return pl.pallas_call(
        functools.partial(prefix_kernel, count=count, per=per, tile=tile),
        grid_spec=pltpu.PrefetchScalarGridSpec(
            num_scalar_prefetch=1,
            grid=(4 * count // per,),
            in_specs=[pl.BlockSpec(qs[0].shape, lambda i, at: (0, 0, 0))] * count
            + [pl.BlockSpec(kv.shape, lambda i, at: (0, 0, 0, 0))]
            + [pl.BlockSpec((4, PACK, HD), lambda i, at: (0, 0, 0))] * len(done),
            out_specs=pl.BlockSpec((blocks, PACK, HD), lambda i, at: (0, 0, 0)),
            scratch_shapes=[pltpu.VMEM((4 * count, ROWS, HD), BF16)],
        ),
        out_shape=jax.ShapeDtypeStruct((blocks, PACK, HD), BF16),
        compiler_params=pltpu.CompilerParams(vmem_limit_bytes=48 << 20),
        cost_estimate=pl.CostEstimate(
            flops=count * ROWS * tokens * HD * 32,
            bytes_accessed=8 << 20,
            transcendentals=count * ROWS * tokens * 4,
        ),
        name="prefix_part",
    )(at, *qs, kv, *done)


def prep_kernel(table_ref, size_ref, q_ref, kv_ref, asked_ref, rows_ref, dealt_ref):
    for c in range(GQA):
        tile = q_ref[:, :, c * HD : (c + 1) * HD].reshape(RS, HD)
        asked_ref[0, c * RS : (c + 1) * RS, :] = tile
        rows_ref[0, c * RS : (c + 1) * RS, :] = tile
    both = kv_ref[0].astype(F32)
    for i in range(2):
        half = both[:, i].astype(BF16)
        dealt_ref[0, 0, i] = half
        dealt_ref[1, 0, i] = half

    @pl.when(pl.program_id(0) == 0)
    def _():
        lane = lax.broadcasted_iota(jnp.int32, (16, HD), 1)
        row = lax.broadcasted_iota(jnp.int32, (16, HD), 0)
        notes = jnp.zeros((16, HD), jnp.int32)
        for slot in range(REQ * MAXP):
            req, page = divmod(slot, MAXP)
            alive = jnp.clip(size_ref[0:1, req : req + 1] - page * PAGE, 0, PAGE)
            here = jnp.where(row == 0, req, jnp.where(row == 1, alive, 0))
            notes = jnp.where(lane == table_ref[0:1, slot : slot + 1], here, notes)
        asked_ref[0, ROWS:, :] = notes.astype(F32).astype(BF16)

    @pl.when(pl.program_id(0) != 0)
    def _():
        asked_ref[0, ROWS:, :] = jnp.zeros((16, HD), BF16)


def prep(page_table, unique_len, queries, prefix_kv):
    tokens = prefix_kv.shape[1]
    return pl.pallas_call(
        prep_kernel,
        grid=(KVH,),
        in_specs=[
            pl.BlockSpec(page_table.shape, lambda k: (0, 0)),
            pl.BlockSpec((1, REQ), lambda k: (0, 0)),
            pl.BlockSpec((REQ, STEPS, GQA * HD), lambda k: (0, 0, k)),
            pl.BlockSpec((1, tokens, 2, HD), lambda k: (0, 0, 0, k)),
        ],
        out_specs=[
            pl.BlockSpec((1, PACK, HD), lambda k: (k, 0, 0)),
            pl.BlockSpec((1, ROWS, HD), lambda k: (k, 0, 0)),
            pl.BlockSpec((2, 1, 2, tokens, HD), lambda k: (0, k, 0, 0, 0)),
        ],
        out_shape=[
            jax.ShapeDtypeStruct((KVH, PACK, HD), BF16),
            jax.ShapeDtypeStruct((KVH, ROWS, HD), BF16),
            jax.ShapeDtypeStruct((2, KVH, 2, tokens, HD), BF16),
        ],
        compiler_params=pltpu.CompilerParams(vmem_limit_bytes=60 << 20),
        name="prep",
    )(page_table, unique_len.reshape(1, REQ), queries, prefix_kv)


def pick_kernel(at_ref, *refs):
    q_refs, out_refs = refs[:4], refs[4:]
    for k, out_ref in enumerate(out_refs):
        head = lax.rem(at_ref[1] + 4 - k, 4)
        for n, q_ref in enumerate(q_refs):
            out_ref[n] = q_ref[head]


def pick(at, asked):
    scalar = pl.BlockSpec(memory_space=pltpu.SMEM)
    whole = pl.BlockSpec(memory_space=pltpu.VMEM)
    return pl.pallas_call(
        pick_kernel,
        in_specs=[scalar] + [whole] * 4,
        out_specs=[whole] * 4,
        out_shape=[jax.ShapeDtypeStruct((4, ROWS, HD), BF16)] * 4,
        compiler_params=pltpu.CompilerParams(vmem_limit_bytes=32 << 20),
        name="pick",
    )(at, *asked)


def page_kernel(at_ref, slot_ref, *refs, first):
    count = (len(refs) - MAXP - 3) // 2
    q_refs, fresh_ref, pages = refs[:count], refs[count], refs[count + 1 : count + 1 + MAXP]
    out_refs, (held, found) = refs[count + 1 + MAXP : -2], refs[-2:]
    t = pl.program_id(0)

    @pl.when(t == 0)
    def _():
        for n, q_ref in enumerate(q_refs):
            held[n] = q_ref[...]

    row = lax.broadcasted_iota(jnp.int32, (ROWS, PAGE), 0)
    token = lax.broadcasted_iota(jnp.int32, (ROWS, PAGE), 1)
    step = lax.rem(row, RS)
    owner = lax.div(step, STEPS)
    notes = held[t, 0, ROWS:, :].astype(F32)
    place = lax.broadcasted_iota(jnp.int32, (1, HD), 1)
    bounds = []
    for c in range(MAXP):
        here = place == at_ref[2] * MAXP + c
        req, size = (
            jnp.sum(jnp.where(here, notes[i : i + 1], 0.0), axis=1, keepdims=True).astype(jnp.int32)
            for i in range(2)
        )
        bounds.append(jnp.where(owner == req, size, 0))

    def attend(own):
        scores, vals = [], []
        for k in range(KVH):
            cols = slice(k * HD, (k + 1) * HD)
            keys = [page[0, 0, :, cols] for page in pages]
            values = [page[0, 1, :, cols] for page in pages]
            if own:
                keys.append(fresh_ref[0, :, cols])
                values.append(fresh_ref[1, :, cols])
            scores.append(dot_t(held[t, k, :ROWS, :], jnp.concatenate(keys, axis=0)))
            vals.append(jnp.concatenate(values, axis=0))
        if own:
            fresh_alive = (
                (lax.div(token, STEPS) == owner)
                & (lax.rem(token, STEPS) <= lax.rem(step, STEPS))
                & (token < RS)
            )
        weights = []
        for s in scores:
            parts = [
                jnp.where(token < bounds[c], s[:, c * PAGE : (c + 1) * PAGE], LOWEST)
                for c in range(MAXP)
            ]
            if own:
                parts.append(jnp.where(fresh_alive, s[:, MAXP * PAGE :], LOWEST))
            top = jnp.max(functools.reduce(jnp.maximum, parts), axis=-1, keepdims=True)
            m = jnp.maximum(jnp.broadcast_to(top, (ROWS, HD)), FLOOR) * LOG2
            p = [jnp.exp2(part * LOG2 - m).astype(BF16) for part in parts]
            weights.append((m, jnp.concatenate(p, axis=1)))
        for k, ((m, p), v) in enumerate(zip(weights, vals)):
            pv = jnp.dot(
                p,
                jnp.concatenate([v, jnp.ones_like(v)], axis=1),
                preferred_element_type=F32,
            )
            found[k, :ROWS, :] = pv[:, :HD].astype(BF16)
            found[k, ROWS:, :] = pack_stats(m, pv[:, HD:])

    if first:
        attend(False)
    else:

        @pl.when(t == 0)
        def _():
            attend(True)

        @pl.when(t != 0)
        def _():
            attend(False)

    for n, out_ref in enumerate(out_refs):

        @pl.when(t == n)
        def _():
            out_ref[...] = found[...]


def page_part(at, slots, asked, first, fresh, pool):
    n = len(asked)

    def page_spec(c):
        return pl.BlockSpec(
            (1, 2, PAGE, KVH * HD),
            lambda t, at, slot: (slot[0, (at[2] ^ (first + t)) * MAXP + c], 0, 0, 0),
        )

    return pl.pallas_call(
        functools.partial(page_kernel, first=first),
        grid_spec=pltpu.PrefetchScalarGridSpec(
            num_scalar_prefetch=2,
            grid=(n,),
            in_specs=[pl.BlockSpec(asked[0].shape, lambda t, at, slot: (0, 0, 0))] * n
            + [pl.BlockSpec(fresh.shape, lambda t, at, slot: (0, 0, 0))]
            + [page_spec(c) for c in range(MAXP)],
            out_specs=[pl.BlockSpec((KVH, PACK, HD), lambda t, at, slot: (0, 0, 0))] * n,
            scratch_shapes=[
                pltpu.VMEM((n, *asked[0].shape), BF16),
                pltpu.VMEM((KVH, PACK, HD), BF16),
            ],
        ),
        out_shape=[jax.ShapeDtypeStruct((KVH, PACK, HD), BF16)] * n,
        compiler_params=pltpu.CompilerParams(vmem_limit_bytes=48 << 20),
        cost_estimate=pl.CostEstimate(
            flops=n * KVH * ROWS * MAXP * PAGE * HD * 64,
            bytes_accessed=4 << 20,
            transcendentals=n * KVH * ROWS * MAXP * PAGE,
        ),
        name="page_part",
    )(at, slots, *asked, fresh, *([pool] * MAXP))


def weigh(stats):
    top = functools.reduce(jnp.maximum, [m for m, _ in stats])
    fades = [jnp.exp2(m - top) for m, _ in stats]
    weight_sum = functools.reduce(jnp.add, [l * f for (_, l), f in zip(stats, fades)])
    return top, fades, weight_sum


def gather_up(gains, values):
    tall = jnp.concatenate([*gains, jnp.zeros((128 - len(gains), 128), F32)], axis=0).T
    total = jnp.zeros((128, HD), F32)
    for i, value in enumerate(values):
        total = total + value.astype(F32) * jnp.broadcast_to(tall[:, i : i + 1], (128, HD))
    return total


def merge_kernel(part_ref, *rest):
    page_refs, o_ref, stat_ref = rest[:-2], rest[-2], rest[-1]
    for head in range(part_ref.shape[0]):
        found = [part_ref.at[head, i] for i in range(part_ref.shape[1])]
        found += [ref.at[head] for ref in page_refs]
        rows = []
        for half in range(ROWS // 128):
            top, fades, weight_sum = weigh([unpack_stats(ref[ROWS:, :], half) for ref in found])
            span = slice(half * 128, half * 128 + 128)
            o_ref[head, span, :] = gather_up(fades, [ref[span, :] for ref in found])
            rows += [top, weight_sum]
        stat_ref[head] = jnp.concatenate([*rows, jnp.zeros((4, 128), F32)], axis=0)


def last_kernel(o_ref, stat_ref, page_ref, out_ref):
    for head in range(o_ref.shape[0]):
        for half in range(ROWS // 128):
            span = slice(half * 128, half * 128 + 128)
            known = stat_ref[head, 2 * half : 2 * half + 1], stat_ref[head, 2 * half + 1 : 2 * half + 2]
            _, fades, weight_sum = weigh([known, unpack_stats(page_ref[head, ROWS:, :], half)])
            gains = [f / weight_sum for f in fades]
            total = gather_up(gains, [o_ref[head, span, :], page_ref[head, span, :]]).astype(BF16)
            for j in range(128 // RS):
                col = head * GQA + half * 128 // RS + j
                rows = total[j * RS : (j + 1) * RS].reshape(REQ, STEPS, HD)
                out_ref[:, :, col * HD : (col + 1) * HD] = rows


def merge(parts, pages, last):
    heads = 2
    steps = (KVH // heads,)
    page = pl.BlockSpec((heads, PACK, HD), lambda k: (k, 0, 0))
    known = [
        pl.BlockSpec((heads, ROWS, HD), lambda k: (k, 0, 0)),
        pl.BlockSpec((heads, 8, HD), lambda k: (k, 0, 0)),
    ]
    params = pltpu.CompilerParams(vmem_limit_bytes=32 << 20)
    o, stats = pl.pallas_call(
        merge_kernel,
        grid=steps,
        in_specs=[pl.BlockSpec((heads, *parts.shape[1:]), lambda k: (k, 0, 0, 0))]
        + [page] * len(pages),
        out_specs=known,
        out_shape=[
            jax.ShapeDtypeStruct((KVH, ROWS, HD), F32),
            jax.ShapeDtypeStruct((KVH, 8, HD), F32),
        ],
        compiler_params=params,
        name="merge",
    )(parts, *pages)
    return pl.pallas_call(
        last_kernel,
        grid=steps,
        in_specs=[*known, page],
        out_specs=pl.BlockSpec((REQ, STEPS, heads * GQA * HD), lambda k: (0, 0, k)),
        out_shape=jax.ShapeDtypeStruct((REQ, STEPS, HQ * HD), BF16),
        compiler_params=params,
        name="merge_last",
    )(o, stats, last)


def swap(x, axis, mask):
    return lax.ppermute(x, axis, [(i, i ^ mask) for i in range(lax.axis_size(axis))])


def fetch(x, axis, by):
    n = lax.axis_size(axis)
    return lax.ppermute(x, axis, [((i + by) % n, i) for i in range(n)])


def after(x, *done):
    return lax.optimization_barrier((x, *done))[0]


def local(queries, prefix_kv, pool, new_kv, unique_len, page_table, send_slots):
    at = jnp.stack([lax.axis_index(name) for name in ("y", "z", "grp")])
    asked, rows, dealt = prep(page_table, unique_len, queries, prefix_kv)
    tokens = prefix_kv.shape[1]
    dealt = dealt.reshape(2 * KVH, 2, tokens, HD)
    kv_all = lax.all_to_all(dealt, ("xl", "z"), 0, 0, tiled=True)
    chunks = [rows] + [fetch(rows, "y", k) for k in (1, 2, 3)]
    asked_1 = swap(asked, "grp", 1)
    fresh = new_kv.transpose(2, 0, 1, 3).reshape(2, RS, KVH * HD)
    fresh = jnp.pad(fresh, ((0, 0), (0, PAGE - RS), (0, 0)))
    near = page_part(at, send_slots, [asked, asked_1], 0, fresh, pool)
    mine, *sent = pick(after(at, near[0]), chunks)
    came = [fetch(x, "z", k) for k, x in enumerate(sent, 1)]
    asked_2 = swap(after(asked, mine), "grp", 2)
    asked_3 = swap(after(asked_1, mine), "grp", 2)
    part = prefix_part(at, [mine], kv_all, [], 4, 256)
    part = prefix_part(at, came, kv_all, [part], 6, 256)
    part = after(part, asked_2, asked_3)
    moved = lax.all_to_all(part, ("z", "y"), 0, 0, tiled=True)
    late = after(at, part)
    (page_2,) = page_part(late, send_slots, [asked_2], 2, fresh, pool)
    (page_3,) = page_part(late, send_slots, [asked_3], 3, fresh, pool)
    pages = [near[0], swap(near[1], "grp", 1), swap(page_2, "grp", 2)]
    return merge(moved.reshape(KVH, 4, PACK, HD), pages, swap(page_3, "grp", 3))


def solution(mesh):
    fine = Mesh(mesh.devices.reshape(4, 4, 2, 4), AXES)
    every = P(AXES)
    dev = ("y", "xl", "z")
    placed = (every, P("grp", dev), every, every, every, every, every)
    return jax.shard_map(local, mesh=fine, in_specs=placed, out_specs=every, check_vma=False)
```

```python
import functools
import math

import jax
import jax.numpy as jnp
from jax import lax
from jax.experimental import pallas as pl
from jax.experimental.pallas import tpu as pltpu
from jax.sharding import Mesh, PartitionSpec as P

HQ = 64
KVH = 4
HD = 128
GQA = 16
STEPS = 4
PAGE = 128
MAXP = 6
REQ = 4
RS = REQ * STEPS
ROWS = RS * GQA
PACK = ROWS + 16
FLOOR = -1e29
HEADS = 2
LOWEST = -1e30
LOG2 = math.log2(math.e) / math.sqrt(HD)
AXES = ("grp", "y", "xl", "z")
F32 = jnp.float32
BF16 = jnp.bfloat16


def dot_t(a, b):
    return lax.dot_general(a, b, (((1,), (1,)), ((), ())), preferred_element_type=F32)


def split3(x):
    hi = x.astype(BF16).astype(F32)
    rest = x - hi
    mid = rest.astype(BF16).astype(F32)
    return hi, mid, rest - mid


def pack_stats(m, l):
    lane = lax.broadcasted_iota(jnp.int32, (128, 128), 1)
    row = lax.broadcasted_iota(jnp.int32, (8, 128), 0)
    parts = []
    for half in range(ROWS // 128):
        rows = slice(half * 128, half * 128 + 128)
        both = jnp.where(lane < 64, m[rows], l[rows]).T
        stats = jnp.zeros((8, 128), F32)
        for i, found in enumerate(split3(both[:8]) + split3(both[64:72])):
            stats = jnp.where(row == i, found, stats)
        parts.append(stats)
    return jnp.concatenate(parts, axis=0).astype(BF16)


def unpack_stats(packed, half):
    wide = packed.astype(F32)[half * 8 : half * 8 + 8]
    return wide[0:1] + wide[1:2] + wide[2:3], wide[3:4] + wide[4:5] + wide[5:6]


def widen(x, width):
    return jnp.concatenate([x] * (width // HD), axis=1)


def scaled(q):
    wide = q.astype(F32) * LOG2
    high = wide.astype(BF16)
    return jnp.concatenate([high, (wide - high.astype(F32)).astype(BF16)], axis=1)


def online(q, kv_ref, tile):
    m = l = o = None
    q = scaled(q)
    blocks, _, tokens, _ = kv_ref.shape
    for b in range(blocks):
        for t in range(0, tokens, tile):
            k = kv_ref[b, 0, t : t + tile, :]
            v = kv_ref[b, 1, t : t + tile, :]
            s = dot_t(q, jnp.concatenate([k, k], axis=1))
            top = jnp.broadcast_to(jnp.max(s, axis=-1, keepdims=True), (q.shape[0], HD))
            new = top if m is None else jnp.maximum(m, top)
            p = jnp.exp2(s - widen(new, tile))
            pv = jnp.dot(
                p.astype(BF16),
                jnp.concatenate([v, jnp.ones_like(v)], axis=1),
                preferred_element_type=F32,
            )
            if m is None:
                l, o = pv[:, HD:], pv[:, :HD]
            else:
                fade = jnp.exp2(m - new)
                l, o = l * fade + pv[:, HD:], o * fade + pv[:, :HD]
            m = new
    return m, l, o


def prefix_kernel(at_ref, *refs, count, per, tile):
    q_refs, kv_ref, done_refs, (out_ref, held) = (
        refs[:count],
        refs[count],
        refs[count + 1 : -2],
        refs[-2:],
    )
    i = pl.program_id(0)
    first = len(done_refs)

    @pl.when(i == 0)
    def _():
        for n, q_ref in enumerate(q_refs):
            held[4 * n : 4 * n + 4] = q_ref[...]
        for done_ref in done_refs:
            for n in range(4):
                out_ref[4 * at_ref[1] + n] = done_ref[n]

    rows = held[pl.ds(i * per, per)].reshape(per * ROWS, HD)
    m, l, o = online(rows, kv_ref, tile)
    for n in range(per):
        part = slice(n * ROWS, (n + 1) * ROWS)
        block = i * per + n
        place = lax.rem(at_ref[0] + block, 4)
        if first:
            place = place + 4 * lax.rem(at_ref[1] + 1 + lax.div(block, 4), 4)
        out_ref[place, :ROWS, :] = o[part].astype(BF16)
        out_ref[place, ROWS:, :] = pack_stats(m[part], l[part])


def prefix_part(at, qs, kv, done, per, tile):
    count = len(qs)
    blocks = 16 if done else 4
    tokens = kv.shape[0] * kv.shape[2]
    return pl.pallas_call(
        functools.partial(prefix_kernel, count=count, per=per, tile=tile),
        grid_spec=pltpu.PrefetchScalarGridSpec(
            num_scalar_prefetch=1,
            grid=(4 * count // per,),
            in_specs=[pl.BlockSpec(qs[0].shape, lambda i, at: (0, 0, 0))] * count
            + [pl.BlockSpec(kv.shape, lambda i, at: (0, 0, 0, 0))]
            + [pl.BlockSpec((4, PACK, HD), lambda i, at: (0, 0, 0))] * len(done),
            out_specs=pl.BlockSpec((blocks, PACK, HD), lambda i, at: (0, 0, 0)),
            scratch_shapes=[pltpu.VMEM((4 * count, ROWS, HD), BF16)],
        ),
        out_shape=jax.ShapeDtypeStruct((blocks, PACK, HD), BF16),
        compiler_params=pltpu.CompilerParams(vmem_limit_bytes=48 << 20),
        cost_estimate=pl.CostEstimate(
            flops=count * ROWS * tokens * HD * 32,
            bytes_accessed=8 << 20,
            transcendentals=count * ROWS * tokens * 4,
        ),
        name="prefix_part",
    )(at, *qs, kv, *done)


def prep_kernel(table_ref, size_ref, q_ref, kv_ref, asked_ref, rows_ref, dealt_ref):
    for head in range(HEADS):
        for c in range(GQA):
            col = (head * GQA + c) * HD
            tile = q_ref[:, :, col : col + HD].reshape(RS, HD)
            asked_ref[head, c * RS : (c + 1) * RS, :] = tile
            rows_ref[head, c * RS : (c + 1) * RS, :] = tile
        both = kv_ref[0, :, :, head * HD : (head + 1) * HD].astype(F32)
        for i in range(2):
            half = both[:, i].astype(BF16)
            dealt_ref[0, head, i] = half
            dealt_ref[1, head, i] = half
        if head:
            asked_ref[head, ROWS:, :] = jnp.zeros((16, HD), BF16)

    @pl.when(pl.program_id(0) == 0)
    def _():
        lane = lax.broadcasted_iota(jnp.int32, (16, HD), 1)
        row = lax.broadcasted_iota(jnp.int32, (16, HD), 0)
        notes = jnp.zeros((16, HD), jnp.int32)
        for slot in range(REQ * MAXP):
            req, page = divmod(slot, MAXP)
            alive = jnp.clip(size_ref[0:1, req : req + 1] - page * PAGE, 0, PAGE)
            here = jnp.where(row == 0, req, jnp.where(row == 1, alive, 0))
            notes = jnp.where(lane == table_ref[0:1, slot : slot + 1], here, notes)
        asked_ref[0, ROWS:, :] = notes.astype(F32).astype(BF16)

    @pl.when(pl.program_id(0) != 0)
    def _():
        asked_ref[0, ROWS:, :] = jnp.zeros((16, HD), BF16)


def prep(page_table, unique_len, queries, prefix_kv):
    tokens = prefix_kv.shape[1]
    return pl.pallas_call(
        prep_kernel,
        grid=(KVH // HEADS,),
        in_specs=[
            pl.BlockSpec(page_table.shape, lambda k: (0, 0)),
            pl.BlockSpec((1, REQ), lambda k: (0, 0)),
            pl.BlockSpec((REQ, STEPS, HEADS * GQA * HD), lambda k: (0, 0, k)),
            pl.BlockSpec((1, tokens, 2, HEADS * HD), lambda k: (0, 0, 0, k)),
        ],
        out_specs=[
            pl.BlockSpec((HEADS, PACK, HD), lambda k: (k, 0, 0)),
            pl.BlockSpec((HEADS, ROWS, HD), lambda k: (k, 0, 0)),
            pl.BlockSpec((2, HEADS, 2, tokens, HD), lambda k: (0, k, 0, 0, 0)),
        ],
        out_shape=[
            jax.ShapeDtypeStruct((KVH, PACK, HD), BF16),
            jax.ShapeDtypeStruct((KVH, ROWS, HD), BF16),
            jax.ShapeDtypeStruct((2, KVH, 2, tokens, HD), BF16),
        ],
        compiler_params=pltpu.CompilerParams(vmem_limit_bytes=60 << 20),
        name="prep",
    )(page_table, unique_len.reshape(1, REQ), queries, prefix_kv)


def pick_kernel(at_ref, *refs):
    q_refs, out_refs = refs[:4], refs[4:]
    for k, out_ref in enumerate(out_refs):
        head = lax.rem(at_ref[1] + 4 - k, 4)
        for n, q_ref in enumerate(q_refs):
            out_ref[n] = q_ref[head]


def pick(at, asked):
    scalar = pl.BlockSpec(memory_space=pltpu.SMEM)
    whole = pl.BlockSpec(memory_space=pltpu.VMEM)
    return pl.pallas_call(
        pick_kernel,
        in_specs=[scalar] + [whole] * 4,
        out_specs=[whole] * 4,
        out_shape=[jax.ShapeDtypeStruct((4, ROWS, HD), BF16)] * 4,
        compiler_params=pltpu.CompilerParams(vmem_limit_bytes=32 << 20),
        name="pick",
    )(at, *asked)


def page_kernel(at_ref, slot_ref, *refs, first):
    count = (len(refs) - MAXP - 3) // 2
    q_refs, fresh_ref, pages = refs[:count], refs[count], refs[count + 1 : count + 1 + MAXP]
    out_refs, (held, found) = refs[count + 1 + MAXP : -2], refs[-2:]
    t = pl.program_id(0)

    @pl.when(t == 0)
    def _():
        for n, q_ref in enumerate(q_refs):
            held[n] = q_ref[...]

    row = lax.broadcasted_iota(jnp.int32, (ROWS, PAGE), 0)
    token = lax.broadcasted_iota(jnp.int32, (ROWS, PAGE), 1)
    step = lax.rem(row, RS)
    owner = lax.div(step, STEPS)
    notes = held[t, 0, ROWS:, :].astype(F32)
    place = lax.broadcasted_iota(jnp.int32, (1, HD), 1)
    bounds = []
    for c in range(MAXP):
        here = place == at_ref[2] * MAXP + c
        req, size = (
            jnp.sum(jnp.where(here, notes[i : i + 1], 0.0), axis=1, keepdims=True).astype(jnp.int32)
            for i in range(2)
        )
        bounds.append(jnp.where(owner == req, size, 0))

    def attend(own):
        scores, vals = [], []
        for k in range(KVH):
            cols = slice(k * HD, (k + 1) * HD)
            keys = [page[0, 0, :, cols] for page in pages]
            values = [page[0, 1, :, cols] for page in pages]
            if own:
                keys.append(fresh_ref[0, :, cols])
                values.append(fresh_ref[1, :, cols])
            scores.append(dot_t(held[t, k, :ROWS, :], jnp.concatenate(keys, axis=0)))
            vals.append(jnp.concatenate(values, axis=0))
        if own:
            fresh_alive = (
                (lax.div(token, STEPS) == owner)
                & (lax.rem(token, STEPS) <= lax.rem(step, STEPS))
                & (token < RS)
            )
        weights = []
        for s in scores:
            parts = [
                jnp.where(token < bounds[c], s[:, c * PAGE : (c + 1) * PAGE], LOWEST)
                for c in range(MAXP)
            ]
            if own:
                parts.append(jnp.where(fresh_alive, s[:, MAXP * PAGE :], LOWEST))
            top = jnp.max(functools.reduce(jnp.maximum, parts), axis=-1, keepdims=True)
            m = jnp.maximum(jnp.broadcast_to(top, (ROWS, HD)), FLOOR) * LOG2
            p = [jnp.exp2(part * LOG2 - m).astype(BF16) for part in parts]
            weights.append((m, jnp.concatenate(p, axis=1)))
        for k, ((m, p), v) in enumerate(zip(weights, vals)):
            pv = jnp.dot(
                p,
                jnp.concatenate([v, jnp.ones_like(v)], axis=1),
                preferred_element_type=F32,
            )
            found[k, :ROWS, :] = pv[:, :HD].astype(BF16)
            found[k, ROWS:, :] = pack_stats(m, pv[:, HD:])

    if first:
        attend(False)
    else:

        @pl.when(t == 0)
        def _():
            attend(True)

        @pl.when(t != 0)
        def _():
            attend(False)

    for n, out_ref in enumerate(out_refs):

        @pl.when(t == n)
        def _():
            out_ref[...] = found[...]


def page_part(at, slots, asked, first, fresh, pool):
    n = len(asked)

    def page_spec(c):
        return pl.BlockSpec(
            (1, 2, PAGE, KVH * HD),
            lambda t, at, slot: (slot[0, (at[2] ^ (first + t)) * MAXP + c], 0, 0, 0),
        )

    return pl.pallas_call(
        functools.partial(page_kernel, first=first),
        grid_spec=pltpu.PrefetchScalarGridSpec(
            num_scalar_prefetch=2,
            grid=(n,),
            in_specs=[pl.BlockSpec(asked[0].shape, lambda t, at, slot: (0, 0, 0))] * n
            + [pl.BlockSpec(fresh.shape, lambda t, at, slot: (0, 0, 0))]
            + [page_spec(c) for c in range(MAXP)],
            out_specs=[pl.BlockSpec((KVH, PACK, HD), lambda t, at, slot: (0, 0, 0))] * n,
            scratch_shapes=[
                pltpu.VMEM((n, *asked[0].shape), BF16),
                pltpu.VMEM((KVH, PACK, HD), BF16),
            ],
        ),
        out_shape=[jax.ShapeDtypeStruct((KVH, PACK, HD), BF16)] * n,
        compiler_params=pltpu.CompilerParams(vmem_limit_bytes=48 << 20),
        cost_estimate=pl.CostEstimate(
            flops=n * KVH * ROWS * MAXP * PAGE * HD * 64,
            bytes_accessed=4 << 20,
            transcendentals=n * KVH * ROWS * MAXP * PAGE,
        ),
        name="page_part",
    )(at, slots, *asked, fresh, *([pool] * MAXP))


def weigh(stats):
    top = functools.reduce(jnp.maximum, [m for m, _ in stats])
    fades = [jnp.exp2(m - top) for m, _ in stats]
    weight_sum = functools.reduce(jnp.add, [l * f for (_, l), f in zip(stats, fades)])
    return top, fades, weight_sum


def gather_up(gains, values):
    tall = jnp.concatenate([*gains, jnp.zeros((128 - len(gains), 128), F32)], axis=0).T
    total = jnp.zeros((128, HD), F32)
    for i, value in enumerate(values):
        total = total + value.astype(F32) * jnp.broadcast_to(tall[:, i : i + 1], (128, HD))
    return total


def merge_kernel(part_ref, *rest):
    page_refs, o_ref, stat_ref = rest[:-2], rest[-2], rest[-1]
    for head in range(part_ref.shape[0]):
        found = [part_ref.at[head, i] for i in range(part_ref.shape[1])]
        found += [ref.at[head] for ref in page_refs]
        rows = []
        for half in range(ROWS // 128):
            top, fades, weight_sum = weigh([unpack_stats(ref[ROWS:, :], half) for ref in found])
            span = slice(half * 128, half * 128 + 128)
            o_ref[head, span, :] = gather_up(fades, [ref[span, :] for ref in found])
            rows += [top, weight_sum]
        stat_ref[head] = jnp.concatenate([*rows, jnp.zeros((4, 128), F32)], axis=0)


def last_kernel(o_ref, stat_ref, page_ref, out_ref):
    for head in range(o_ref.shape[0]):
        for half in range(ROWS // 128):
            span = slice(half * 128, half * 128 + 128)
            known = stat_ref[head, 2 * half : 2 * half + 1], stat_ref[head, 2 * half + 1 : 2 * half + 2]
            _, fades, weight_sum = weigh([known, unpack_stats(page_ref[head, ROWS:, :], half)])
            gains = [f / weight_sum for f in fades]
            total = gather_up(gains, [o_ref[head, span, :], page_ref[head, span, :]]).astype(BF16)
            for j in range(128 // RS):
                col = head * GQA + half * 128 // RS + j
                rows = total[j * RS : (j + 1) * RS].reshape(REQ, STEPS, HD)
                out_ref[:, :, col * HD : (col + 1) * HD] = rows


def merge(parts, pages, last):
    heads = 2
    steps = (KVH // heads,)
    page = pl.BlockSpec((heads, PACK, HD), lambda k: (k, 0, 0))
    known = [
        pl.BlockSpec((heads, ROWS, HD), lambda k: (k, 0, 0)),
        pl.BlockSpec((heads, 8, HD), lambda k: (k, 0, 0)),
    ]
    params = pltpu.CompilerParams(vmem_limit_bytes=32 << 20)
    o, stats = pl.pallas_call(
        merge_kernel,
        grid=steps,
        in_specs=[pl.BlockSpec((heads, *parts.shape[1:]), lambda k: (k, 0, 0, 0))]
        + [page] * len(pages),
        out_specs=known,
        out_shape=[
            jax.ShapeDtypeStruct((KVH, ROWS, HD), F32),
            jax.ShapeDtypeStruct((KVH, 8, HD), F32),
        ],
        compiler_params=params,
        name="merge",
    )(parts, *pages)
    return pl.pallas_call(
        last_kernel,
        grid=steps,
        in_specs=[*known, page],
        out_specs=pl.BlockSpec((REQ, STEPS, heads * GQA * HD), lambda k: (0, 0, k)),
        out_shape=jax.ShapeDtypeStruct((REQ, STEPS, HQ * HD), BF16),
        compiler_params=params,
        name="merge_last",
    )(o, stats, last)


def swap(x, axis, mask):
    return lax.ppermute(x, axis, [(i, i ^ mask) for i in range(lax.axis_size(axis))])


def fetch(x, axis, by):
    n = lax.axis_size(axis)
    return lax.ppermute(x, axis, [((i + by) % n, i) for i in range(n)])


def after(x, *done):
    return lax.optimization_barrier((x, *done))[0]


def local(queries, prefix_kv, pool, new_kv, unique_len, page_table, send_slots):
    at = jnp.stack([lax.axis_index(name) for name in ("y", "z", "grp")])
    asked, rows, dealt = prep(page_table, unique_len, queries, prefix_kv)
    tokens = prefix_kv.shape[1]
    dealt = dealt.reshape(2 * KVH, 2, tokens, HD)
    kv_all = lax.all_to_all(dealt, ("xl", "z"), 0, 0, tiled=True)
    chunks = [rows] + [fetch(rows, "y", k) for k in (1, 2, 3)]
    asked_1 = swap(asked, "grp", 1)
    fresh = new_kv.transpose(2, 0, 1, 3).reshape(2, RS, KVH * HD)
    fresh = jnp.pad(fresh, ((0, 0), (0, PAGE - RS), (0, 0)))
    near = page_part(at, send_slots, [asked, asked_1], 0, fresh, pool)
    mine, *sent = pick(after(at, near[0]), chunks)
    came = [fetch(x, "z", k) for k, x in enumerate(sent, 1)]
    asked_2 = swap(after(asked, mine), "grp", 2)
    asked_3 = swap(after(asked_1, mine), "grp", 2)
    part = prefix_part(at, [mine], kv_all, [], 4, 256)
    part = prefix_part(at, came, kv_all, [part], 6, 256)
    part = after(part, asked_2, asked_3)
    moved = lax.all_to_all(part, ("z", "y"), 0, 0, tiled=True)
    late = after(at, part)
    (page_2,) = page_part(late, send_slots, [asked_2], 2, fresh, pool)
    (page_3,) = page_part(late, send_slots, [asked_3], 3, fresh, pool)
    pages = [near[0], swap(near[1], "grp", 1), swap(page_2, "grp", 2)]
    return merge(moved.reshape(KVH, 4, PACK, HD), pages, swap(page_3, "grp", 3))


def solution(mesh):
    fine = Mesh(mesh.devices.reshape(4, 4, 2, 4), AXES)
    every = P(AXES)
    dev = ("y", "xl", "z")
    placed = (every, P("grp", dev), every, every, every, every, every)
    return jax.shard_map(local, mesh=fine, in_specs=placed, out_specs=every, check_vma=False)
```
